32 devices in a mesh: dom: 8 (over y, x, core), sub: 4 (over z).
Axes of the slice: x: 2, y: 2, z: 4, core: 2. Of those that a mesh axis runs over, the one named last changes fastest.
Arguments:
- history: bfloat16 [1024, 64, 128], P(('dom', 'sub')), may hold values from -6 to 6
- send_list: int32 [32, 32, 1], P(('dom', 'sub')), may hold values from 0 to 31
- send_count: int32 [32, 32], P(('dom', 'sub')), may hold values from 0 to 1, as said below
- mixed_mass: bfloat16 [1024, 128, 128], P(('dom', 'sub')), may hold values from -0.5 to 0.5
- relay_list: int32 [32, 32, 1], P(('dom', 'sub')), may hold values from 0 to 31, as said below
- relay_target: int32 [32, 32, 1], P(('dom', 'sub')), may hold values from 0 to 63
- mass_diag: float32 [2048, 128, 128], P(('dom', 'sub')), as said below
- mass_next: float32 [2048, 128, 128], P(('dom', 'sub')), may hold values from -0.18 to 0.18
- coupling: int32 [2048], P(('dom', 'sub')), may hold values 0 or 1
- precond: float32 [2048, 128, 128], P(('dom', 'sub')), as said below
Outputs:
- solution: float32 [2048, 64, 128], P(('dom', 'sub'))
- residual: float32 [2048, 64, 128], P(('dom', 'sub'))
The draws below stay inside these ranges and needn't reach their ends.
Inputs may be any that keep to these rules, and one draw needn't show every extreme that they name: `send_count`: live slots are the first ones. Every sender fills all 1 slots for some peer, and in every draw some receiver gets 1 live slots from every sender. For each owner e, the entries of relay_list[e] are a permutation of 0 .. 31. `mass_diag`: each block is symmetric; the assembled mass matrix is symmetric positive definite. `precond`: each block is symmetric positive definite.
All inputs are finite; a program needn't handle non-finite values. No bound on the sum of `coupling` on one device may be relied on, other than what follows from the above.
Results may differ from the reference program's by a relative error of at most 0.0003.
Values may be sent and summed in bfloat16 or wider, within the bound.
No kernel may reach another device: no remote copies, remote signals or barrier semaphores. Data moves between devices by JAX's collectives and lax.ppermute only.
A program may use at most 128 MiB of HBM per device.

```python
import math
import jax
import jax.numpy as jnp
from jax import lax

VALS = 64
BROWS = 128
OB = 32
CAP = 1
NB = 64
ITERS = 3
SB = 32
OLD_BLOCKS = 1024
SLOTS = 1024
NEW_BLOCKS = 2048
DEVICES = 32


def draw_send_count(key, part):
    first_key, second_key, third_key = jax.random.split(key, 3)
    counts = jax.random.randint(first_key, (DEVICES, DEVICES), 0, CAP + 1)
    favoured = jax.random.randint(second_key, (DEVICES, 1), 0, DEVICES)
    column = jax.random.randint(third_key, (), 0, DEVICES)
    peers = jnp.arange(DEVICES)
    counts = jnp.where(peers[None, :] == favoured, CAP, counts)
    counts = jnp.where(peers[None, :] == column, CAP, counts)
    return counts.astype(jnp.int32)


def shuffled(one_key):
    return jax.random.permutation(one_key, DEVICES * CAP)


def draw_relay_list(key, part):
    keys = jax.random.split(key, DEVICES)
    orders = jax.vmap(shuffled)(keys)
    return orders.reshape(DEVICES, DEVICES, CAP).astype(jnp.int32)


def diagonal_rates(key):
    rate_key = jax.random.fold_in(key, 7)
    rates = jnp.exp(jax.random.uniform(rate_key, (NEW_BLOCKS, BROWS), jnp.float32, math.log(3.0), math.log(24.0)))
    return rates


def symmetric_noise(key, salt, scale):
    noise = jax.random.normal(jax.random.fold_in(key, salt), (NEW_BLOCKS, BROWS, BROWS), jnp.float32) * scale
    return (noise + jnp.swapaxes(noise, 1, 2)) * math.sqrt(0.5)


def draw_mass_diag(key, part):
    rates = diagonal_rates(key)
    identity = jnp.eye(BROWS, dtype=jnp.float32)[None]
    return symmetric_noise(key, 11, 0.03) + rates[:, :, None] * identity


def draw_precond(key, part):
    rates = diagonal_rates(key)
    identity = jnp.eye(BROWS, dtype=jnp.float32)[None]
    return symmetric_noise(key, 13, 0.0008) + (1.0 / rates)[:, :, None] * identity


def plant(values, rng, smallest, top_value):
    shape = values.shape
    spot = [jax.random.randint(jax.random.fold_in(rng, axis), (), 0, shape[axis]) for axis in range(len(shape))]
    values = values.at[tuple(spot)].set(smallest)
    longest = shape.index(max(shape))
    spot[longest] = (spot[longest] + 1) % shape[longest]
    return values.at[tuple(spot)].set(top_value)


def shard_levels(own_key, dims, pieces, least, high):
    factor_of = 1.0
    for position, blocks in pieces:
        draws = jax.random.uniform(jax.random.fold_in(jax.random.fold_in(own_key, 6), position), (blocks,), jnp.float32, least / len(pieces), high / len(pieces))
        factor_of = factor_of * jnp.repeat(jnp.exp(draws), dims[position] // blocks).reshape((-1,) + (1,) * (len(dims) - 1 - position))
    return factor_of


def bell_draw(key, shape, spread, limit, pieces=(), held_as=jnp.bfloat16):
    array = jax.random.normal(key, shape, jnp.float32) * spread
    if len(pieces) > 0:
        array = shard_levels(key, shape, pieces, -0.22, 0.18) * array
    return jnp.clip(array, min=-limit, max=limit).astype(held_as)


def setup_inputs(seed: int = 0) -> dict:
    streams_of = jax.random.split(jax.random.key(seed), 11)
    return {
        "history": bell_draw(streams_of[0], (OLD_BLOCKS, VALS, BROWS), 1.0, 6.0, ((0, 32),)),
        "send_list": plant(jax.random.randint(streams_of[1], (DEVICES, DEVICES, CAP), 0, OB), jax.random.fold_in(streams_of[1], 1), 0, OB - 1).astype(jnp.int32),
        "send_count": draw_send_count(jax.random.fold_in(streams_of[10], 71), 0),
        "mixed_mass": bell_draw(streams_of[3], (SLOTS, BROWS, BROWS), BROWS ** -0.5, 0.5, ((0, 32),)),
        "relay_list": draw_relay_list(jax.random.fold_in(streams_of[10], 71), 0),
        "relay_target": plant(jax.random.randint(streams_of[5], (DEVICES, DEVICES, CAP), 0, NB), jax.random.fold_in(streams_of[5], 1), 0, NB - 1).astype(jnp.int32),
        "mass_diag": draw_mass_diag(jax.random.fold_in(streams_of[10], 71), 0),
        "mass_next": bell_draw(streams_of[7], (NEW_BLOCKS, BROWS, BROWS), 0.03, 0.18, ((0, 32),), jnp.float32),
        "coupling": plant((jax.random.randint(streams_of[8], (NEW_BLOCKS,), 0, 4) < 3).astype(jnp.int32), jax.random.fold_in(streams_of[8], 1), 0, 1),
        "precond": draw_precond(jax.random.fold_in(streams_of[10], 71), 0),
    }


def apply_mass(field, mass_diag, mass_next, links):
    highest = lax.Precision.HIGHEST
    carried = links * jnp.einsum('gvs,gsr->gvr', field, mass_next, precision=highest)
    zero_block = jnp.zeros_like(field[:1])
    ahead = jnp.concatenate([field[1:], zero_block], axis=0)
    behind = jnp.concatenate([zero_block, carried[:-1]], axis=0)
    own = jnp.einsum('gvs,grs->gvr', field, mass_diag, precision=highest)
    onward = links * jnp.einsum('gvs,grs->gvr', ahead, mass_next, precision=highest)
    return own + onward + behind


def precondition(field, precond):
    return jnp.einsum('gvs,grs->gvr', field, precond, precision=lax.Precision.HIGHEST)


def reference(history, send_list, send_count, mixed_mass, relay_list, relay_target, mass_diag, mass_next, coupling, precond):
    highest = lax.Precision.HIGHEST
    slot_index = jnp.arange(CAP, dtype=jnp.int32)
    device_index = jnp.arange(DEVICES, dtype=jnp.int32)
    mixing = mixed_mass.reshape(DEVICES, SB, BROWS, BROWS)

    def per_owner(rhs, owner):
        picks = send_list[:, owner, :]
        live = slot_index[None, :] < send_count[:, owner][:, None]
        source = (device_index[:, None] * OB + picks).astype(jnp.int32)
        blocks = jnp.where(live[:, :, None, None], history[source], jnp.zeros((), history.dtype))
        blocks = blocks.reshape(SB, VALS, BROWS).astype(jnp.float32)
        tiles = jnp.einsum('kvs,ksr->kvr', blocks, mixing[owner].astype(jnp.float32), precision=highest)
        sending = tiles[relay_list[owner].reshape(-1).astype(jnp.int32)]
        target = (device_index[:, None] * NB + relay_target[:, owner, :]).astype(jnp.int32)
        rhs = rhs.at[target.reshape(-1)].add(sending)
        return rhs, None

    start = jnp.zeros((NEW_BLOCKS, VALS, BROWS), jnp.float32)
    rhs = lax.scan(per_owner, start, device_index)[0]

    links = coupling.astype(jnp.float32)[:, None, None]
    solution = jnp.zeros_like(rhs)
    residual = rhs
    reduced = precondition(residual, precond)
    direction = reduced
    norm_now = jnp.sum(residual * reduced, axis=(0, 2))
    for iteration in range(ITERS):
        image = apply_mass(direction, mass_diag, mass_next, links)
        alpha = norm_now / jnp.sum(direction * image, axis=(0, 2))
        solution = solution + alpha[None, :, None] * direction
        residual = residual - alpha[None, :, None] * image
        reduced = precondition(residual, precond)
        norm_next = jnp.sum(residual * reduced, axis=(0, 2))
        direction = reduced + (norm_next / norm_now)[None, :, None] * direction
        norm_now = norm_next
    return solution, residual
```

```python
import functools

import jax
import jax.numpy as jnp
from jax import lax
from jax.experimental import pallas as pl
from jax.experimental.pallas import tpu as pltpu
from jax.sharding import PartitionSpec as P

AXES = ("dom", "sub")
EDGE = 3
EXTRA = 16
OCTAVE = 64.0
FULL = 32766.0
TINY = 1e-37
F32 = jnp.float32
BF16 = jnp.bfloat16
WHOLE = pl.BlockSpec(memory_space=pltpu.VMEM)
SCALARS = pl.BlockSpec(memory_space=pltpu.SMEM)


def params(mebibytes):
    return pltpu.CompilerParams(vmem_limit_bytes=mebibytes * 2**20)


def cost(flops, moved):
    return pl.CostEstimate(flops=int(flops), bytes_accessed=int(moved), transcendentals=0)


def dot(first, second):
    return jnp.dot(first, second, preferred_element_type=F32)


def parted(value):
    high = value.astype(BF16)
    return high, (value - high.astype(F32)).astype(BF16)


def tall(value):
    return jnp.concatenate(parted(value), axis=0)


def wide(value):
    return jnp.concatenate(parted(value), axis=1)


def by_wide(stacked, weights):
    rows, columns = stacked.shape[0] // 2, weights.shape[1] // 2
    out = dot(stacked, weights)
    return out[:rows, :columns] + (out[rows:, :columns] + out[:rows, columns:])


def by_pair(stacked, high, low):
    rows = stacked.shape[0] // 2
    out = dot(stacked, high)
    return out[:rows] + (out[rows:] + dot(stacked[:rows], low))


def pick_kernel(picks, counts, history, outgoing, *, slots):
    def step(entry, carry):
        live = (entry % slots) < counts[entry // slots]
        block = history[picks[entry]]
        outgoing[entry] = jnp.where(live, block, jnp.zeros_like(block))
        return carry

    total = outgoing.shape[0]
    lax.fori_loop(0, total, step, 0, unroll=8)


def prepare_kernel(coupling, diag, onward, precond, weights, pair_high, pair_low, cross, cross_t, trace, edges):
    step = pl.program_id(0)
    steps = pl.num_programs(0)
    blocks = diag.shape[0]
    rows = diag.shape[1]
    total = jnp.zeros((rows, rows), F32)
    for local in range(blocks):
        block = step * blocks + local
        own = diag[local]
        pre = precond[local]
        weights[block] = wide(pre)
        total = total + own * pre
    for local in range(blocks // 2):
        pair = step * (blocks // 2) + local
        linked = onward[2 * local] * coupling[2 * pair].astype(F32)
        whole = jnp.concatenate(
            [
                jnp.concatenate([diag[2 * local], linked], axis=1),
                jnp.concatenate([linked.T, diag[2 * local + 1]], axis=1),
            ],
            axis=0,
        )
        high, low = parted(whole)
        pair_high[pair] = high
        pair_low[pair] = low
        after = onward[2 * local + 1] * coupling[2 * pair + 1].astype(F32)
        cross[pair] = wide(after)
        cross_t[pair] = wide(after.T)
    part = total.reshape(rows // 8, 8, rows).sum(axis=0)

    @pl.when(step == 0)
    def _():
        trace[...] = part
        exact = functools.partial(jnp.dot, precision=lax.Precision.HIGHEST, preferred_element_type=F32)
        first = precond[0]
        edges[2] = first
        edges[3] = exact(exact(first, diag[0]), first)

    @pl.when(step > 0)
    def _():
        trace[...] += part

    @pl.when(step == steps - 1)
    def _():
        exact = functools.partial(jnp.dot, precision=lax.Precision.HIGHEST, preferred_element_type=F32)
        last = onward[blocks - 1] * coupling[steps * blocks - 1].astype(F32)
        mapped = exact(precond[blocks - 1], last)
        edges[0] = exact(last.T, mapped)
        edges[1] = exact(mapped.T, exact(diag[blocks - 1], mapped))


def mix_kernel(relay, arrived, mixing, trace, sending):
    total, values, rows = arrived.shape
    entries = trace.shape[0] * trace.shape[1]
    share = jnp.sum(jnp.sum(trace[...], axis=0, keepdims=True), axis=1, keepdims=True)
    share = jnp.maximum(jnp.broadcast_to(share, (1, rows)), TINY)
    share_code = jnp.floor(jnp.log2(share) * OCTAVE).astype(jnp.int32)
    lower = lax.broadcasted_iota(jnp.int32, (EXTRA, rows), 0) < EXTRA // 2

    def step(entry, carry):
        slot = relay[entry]
        tile = dot(arrived[slot], mixing[slot])
        peak = jnp.max(jnp.abs(tile), axis=0, keepdims=True)
        code = jnp.floor(jnp.log2(jnp.maximum(peak, TINY)) * OCTAVE) + 2.0
        scaled = tile * (FULL / jnp.exp2(code * (1.0 / OCTAVE)))
        scaled = jnp.clip(jnp.floor(scaled + 0.5), -32767.0, 32767.0)
        sending[entry, :values] = scaled.astype(jnp.int32).astype(jnp.int16)
        codes = jnp.where(lower, code.astype(jnp.int32), share_code)
        sending[entry, values:] = codes.astype(jnp.int16)
        return carry

    lax.fori_loop(0, total, step, 0, unroll=8)


def assemble_kernel(
    targets, received, weights, pair_high, pair_low, cross, cross_t, edges, rhs, theta_out, to_left, to_right, *, eigens
):
    total = received.shape[0]
    blocks, values, rows = rhs.shape
    rhs[...] = jnp.zeros_like(rhs)

    def step(entry, carry):
        extra = jnp.exp2(received[entry, values:].astype(jnp.int32).astype(F32) * (1.0 / OCTAVE))
        tile = received[entry, :values].astype(jnp.int32).astype(F32) * (extra[:1] * (1.0 / FULL))
        block = targets[entry]
        rhs[block] = rhs[block] + tile
        return carry + extra[EXTRA // 2 :]

    shares = lax.fori_loop(0, total, step, jnp.zeros((EXTRA // 2, rows), F32), unroll=8)
    theta = shares[:1] * (1.0 / eigens)
    theta_out[...] = jnp.broadcast_to(theta, theta_out.shape)
    pairs = blocks // 2

    def pre(value, block):
        return by_wide(tall(value), weights[block])

    both = functools.partial(jnp.concatenate, axis=1)
    first = [rhs[block] for block in range(EDGE)]
    z0 = [pre(first[block], block) for block in range(EDGE)]
    q1 = by_pair(tall(both(z0[:2])), pair_high[0], pair_low[0]) - both([theta, theta]) * both(first[:2])
    q1 = [q1[:, :rows], q1[:, rows:] + by_wide(tall(z0[2]), cross_t[0])]
    z1 = [pre(q1[block], block) for block in range(2)]
    q2 = by_pair(tall(both(z1)), pair_high[0], pair_low[0])[:, :rows] - theta * q1[0]
    to_left[0] = z0[0]
    to_left[1] = z1[0]
    to_left[2] = pre(q2, 0)
    last = [rhs[blocks - EDGE + block] for block in range(EDGE)]
    z0 = [pre(last[block], blocks - EDGE + block) for block in range(EDGE)]
    q1 = by_pair(tall(both(z0[1:])), pair_high[pairs - 1], pair_low[pairs - 1]) - both([theta, theta]) * both(last[1:])
    q1 = [q1[:, :rows] + by_wide(tall(z0[0]), cross[pairs - 2]), q1[:, rows:]]
    z1 = [pre(q1[block], blocks - 2 + block) for block in range(2)]
    q2 = by_pair(tall(both(z1)), pair_high[pairs - 1], pair_low[pairs - 1])[:, rows:] - theta * q1[1]
    for place, value in enumerate((z0[2], z1[1], pre(q2, blocks - 1))):
        to_right[place] = by_wide(tall(value), cross[pairs - 1])
    for half in range(2):
        part = slice(half * values, (half + 1) * values)
        to_right[3 + half] = edges[0, part]
        to_right[5 + half] = edges[1, part]
        to_left[3 + half] = edges[2, part]
        to_left[5 + half] = edges[3, part]


def basis_kernel(rhs, theta_in, weights, pair_high, pair_low, cross, cross_t, basis, mapped, sums, stacked):
    blocks, values, rows = rhs.shape
    pairs = blocks // 2
    theta = theta_in[:1]
    theta_pair = jnp.concatenate([theta, theta], axis=1)
    basis[0] = rhs[...]

    def sweep(level, carry):
        even = jnp.zeros((values, rows), F32)
        for block in range(blocks):
            value = basis[level, block]
            image = by_wide(tall(value), weights[block])
            mapped[level, block] = image
            high, low = parted(image)
            side = slice((block % 2) * rows, (block % 2 + 1) * rows)
            stacked[block // 2, :values, side] = high
            stacked[block // 2, values:, side] = low
            if EDGE <= block < blocks - EDGE:
                even = even + value * image
        sums[2 * level] = even
        odd = jnp.zeros((values, rows), F32)
        for pair in range(pairs):
            image = by_pair(stacked[pair], pair_high[pair], pair_low[pair])
            sides = [image[:, :rows], image[:, rows:]]
            if pair > 0:
                sides[0] = sides[0] + by_wide(stacked[pair - 1, :, rows:], cross[pair - 1])
            if pair < pairs - 1:
                sides[1] = sides[1] + by_wide(stacked[pair + 1, :, :rows], cross_t[pair])
            for side in range(2):
                block = 2 * pair + side
                value = sides[side] - theta * basis[level, block]
                basis[level + 1, block] = value
                if EDGE <= block < blocks - EDGE:
                    odd = odd + value * mapped[level, block]
        sums[2 * level + 1] = odd
        return carry

    lax.fori_loop(0, 3, sweep, 0)


def edge_kernel(
    from_left, from_right, basis, mapped, sums, theta_in, weights, pair_high, pair_low, cross, cross_t,
    basis_edge, mapped_edge, moments,
):
    _, blocks, values, rows = basis.shape
    pairs = blocks // 2
    theta = theta_in[:1]

    def pre(value, block):
        return by_wide(tall(value), weights[block])

    def pair_image(first, second, pair):
        out = by_pair(tall(jnp.concatenate([first, second], axis=1)), pair_high[pair], pair_low[pair])
        return out[:, :rows], out[:, rows:]

    def square(ref, place):
        return jnp.concatenate([ref[place], ref[place + 1]], axis=0)

    none = jnp.zeros((values, rows), F32)

    mirror = square(from_left, 3)
    second = square(from_left, 5) - theta * mirror
    mirror, second = wide(mirror), wide(second)
    start = tall(mapped[0, 0])
    dq1 = from_left[0]
    dz1 = pre(dq1, 0)
    z1 = mapped[1, 0] + dz1
    own, after = pair_image(dz1, none, 0)
    dq2 = (own - theta * dq1 + from_left[1] + by_wide(start, mirror), after)
    dz2 = (pre(dq2[0], 0), pre(dq2[1], 1))
    own, after = pair_image(dz2[0], dz2[1], 0)
    dq3 = (
        own - theta * dq2[0] + from_left[2] + by_wide(start, second) + by_wide(tall(z1), mirror),
        after - theta * dq2[1],
        by_wide(tall(dz2[1]), cross[0]),
    )
    changes = [((0, dq1),), ((0, dq2[0]), (1, dq2[1])), ((0, dq3[0]), (1, dq3[1]), (2, dq3[2]))]
    images = [((0, dz1),), ((0, dz2[0]), (1, dz2[1]))]

    last = blocks - 1
    pair = pairs - 1
    mirror = square(from_right, 3)
    second = square(from_right, 5) - theta * mirror
    mirror, second = wide(mirror), wide(second)
    start = tall(by_wide(tall(mapped[0, last]), cross[pair]))
    dq1 = by_wide(tall(from_right[0]), cross_t[pair])
    dz1 = pre(dq1, last)
    z1 = mapped[1, last] + dz1
    before, own = pair_image(none, dz1, pair)
    ahead = from_right[1] + by_wide(start, mirror)
    dq2 = (own - theta * dq1 + by_wide(tall(ahead), cross_t[pair]), before)
    dz2 = (pre(dq2[0], last), pre(dq2[1], last - 1))
    before, own = pair_image(dz2[1], dz2[0], pair)
    ahead = from_right[2] + by_wide(start, second) + by_wide(tall(by_wide(tall(z1), cross[pair])), mirror)
    dq3 = (
        own - theta * dq2[0] + by_wide(tall(ahead), cross_t[pair]),
        before - theta * dq2[1],
        by_wide(tall(dz2[1]), cross_t[pair - 1]),
    )
    changes[0] += ((5, dq1),)
    changes[1] += ((5, dq2[0]), (4, dq2[1]))
    changes[2] += ((5, dq3[0]), (4, dq3[1]), (3, dq3[2]))
    images[0] += ((5, dz1),)
    images[1] += ((5, dz2[0]), (4, dz2[1]))

    places = [0, 1, 2, blocks - 3, blocks - 2, blocks - 1]
    before = [rhs_block for rhs_block in (basis[0, block] for block in places)]
    lane = lax.broadcasted_iota(jnp.int32, (values, rows), 1)
    table = none
    for level in range(3):
        image = [mapped[level, block] for block in places]
        if level > 0:
            for place, change in images[level - 1]:
                image[place] = image[place] + change
            for place in range(2 * EDGE):
                mapped_edge[level - 1, place] = image[place]
        now = [basis[level + 1, block] for block in places]
        for place, change in changes[level]:
            now[place] = now[place] + change
        even = sums[2 * level]
        odd = sums[2 * level + 1]
        for place in range(2 * EDGE):
            basis_edge[level, place] = now[place]
            even = even + before[place] * image[place]
            odd = odd + now[place] * image[place]
        table = jnp.where(lane == 2 * level, jnp.sum(even, axis=1, keepdims=True), table)
        table = jnp.where(lane == 2 * level + 1, jnp.sum(odd, axis=1, keepdims=True), table)
        before = now
    flipped = jnp.concatenate([table, jnp.zeros((rows - values, rows), F32)], axis=0).T[:8]
    for peer in range(moments.shape[0]):
        moments[peer] = flipped


def combine_kernel(moments, theta_in, basis, mapped, basis_edge, mapped_edge, solution, residual, factors):
    step = pl.program_id(0)
    _, blocks, values, rows = basis.shape
    chunk = solution.shape[0]

    @pl.when(step == 0)
    def _():
        total = jnp.sum(moments[...], axis=0)
        theta = theta_in[:1]
        m0, m1, m2, m3, m4, m5 = (total[place : place + 1] for place in range(6))
        m0 = m0 + TINY
        l10 = m1 / m0
        l20 = m2 / m0
        d1 = m2 - l10 * m1 + TINY
        g21 = m3 - l20 * m1
        l21 = g21 / d1
        d2 = m4 - l20 * m2 - l21 * g21 + TINY
        b1 = l10 * m3 - m4
        b2 = l20 * m3 - l21 * b1 - m5
        c2 = b2 / d2
        c1 = b1 / d1 - l21 * c2
        c0 = -m3 / m0 - l10 * c1 - l20 * c2
        scale = 1.0 / (c0 - theta * (c1 - theta * (c2 - theta)))
        c0, c1, c2, c3 = c0 * scale, c1 * scale, c2 * scale, scale
        y2 = -c3
        y1 = -c2 - theta * y2
        y0 = -c1 - theta * y1
        table = jnp.concatenate([c0, c1, c2, c3, y0, y1, y2, jnp.zeros((rows - 7, rows), F32)], axis=0).T
        for place in range(7):
            factors[place] = jnp.broadcast_to(table[:values, place : place + 1], (values, rows))

    factor = [factors[place] for place in range(7)]

    def store(place, q, z):
        residual[place] = (q[0] * factor[0] + q[1] * factor[1]) + (q[2] * factor[2] + q[3] * factor[3])
        solution[place] = z[0] * factor[4] + z[1] * factor[5] + z[2] * factor[6]

    for place in range(chunk):
        block = step * chunk + place
        store(place, [basis[level, block] for level in range(4)], [mapped[level, block] for level in range(3)])

    def edge(place, block, entry):
        q = [basis[0, block]] + [basis_edge[level, entry] for level in range(3)]
        z = [mapped[0, block]] + [mapped_edge[level, entry] for level in range(2)]
        store(place, q, z)

    @pl.when(step == 0)
    def _():
        for entry in range(EDGE):
            edge(entry, entry, entry)

    @pl.when(step == pl.num_programs(0) - 1)
    def _():
        for entry in range(EDGE):
            edge(chunk - EDGE + entry, blocks - EDGE + entry, EDGE + entry)


def shifted(value, steps):
    count = lax.axis_size(AXES)
    first, last = (max(0, -steps), min(count, count - steps))
    return lax.ppermute(value, AXES, [(source, source + steps) for source in range(first, last)])


def body(
    history,
    send_list,
    send_count,
    mixed_mass,
    relay_list,
    relay_target,
    mass_diag,
    mass_next,
    coupling,
    precond,
):
    devices = lax.axis_size(AXES)
    slots = send_list.shape[2]
    total = devices * slots
    values, rows = history.shape[1:]
    blocks = mass_diag.shape[0]
    pairs = blocks // 2
    field = (blocks, values, rows)
    unit = 2 * values * rows * rows

    outgoing = pl.pallas_call(
        functools.partial(pick_kernel, slots=slots),
        out_shape=jax.ShapeDtypeStruct((total, values, rows), BF16),
        in_specs=[SCALARS, SCALARS, WHOLE],
        out_specs=WHOLE,
        compiler_params=params(16),
        name="pick",
    )(send_list.reshape(-1), send_count.reshape(-1), history)
    arrived = lax.all_to_all(outgoing, AXES, split_axis=0, concat_axis=0, tiled=True)

    chunk = 8
    matrix = pl.BlockSpec((chunk, rows, rows), lambda step: (step, 0, 0))
    weights, pair_high, pair_low, cross, cross_t, trace, edges = pl.pallas_call(
        prepare_kernel,
        grid=(blocks // chunk,),
        out_shape=(
            pltpu.VMEM((blocks, rows, 2 * rows), BF16),
            pltpu.VMEM((pairs, 2 * rows, 2 * rows), BF16),
            pltpu.VMEM((pairs, 2 * rows, 2 * rows), BF16),
            pltpu.VMEM((pairs, rows, 2 * rows), BF16),
            pltpu.VMEM((pairs, rows, 2 * rows), BF16),
            pltpu.VMEM((8, rows), F32),
            pltpu.VMEM((4, rows, rows), F32),
        ),
        in_specs=[SCALARS, matrix, matrix, matrix],
        out_specs=(WHOLE,) * 7,
        compiler_params=params(16),
        cost_estimate=cost(0, 28 * 2**20),
        name="prepare",
    )(coupling, mass_diag, mass_next, precond)
    operator = (weights, pair_high, pair_low, cross, cross_t)

    sending = pl.pallas_call(
        mix_kernel,
        out_shape=jax.ShapeDtypeStruct((total, values + EXTRA, rows), jnp.int16),
        in_specs=[SCALARS, WHOLE, WHOLE, WHOLE],
        out_specs=WHOLE,
        compiler_params=params(16),
        name="mix",
    )(relay_list.reshape(-1), arrived, mixed_mass, trace)
    received = lax.all_to_all(sending, AXES, split_axis=0, concat_axis=0, tiled=True)

    ends = jax.ShapeDtypeStruct((EDGE + 4, values, rows), F32)
    rhs, theta, to_left, to_right = pl.pallas_call(
        functools.partial(assemble_kernel, eigens=devices * blocks * rows),
        out_shape=(pltpu.VMEM(field, F32), pltpu.VMEM((8, rows), F32), ends, ends),
        in_specs=[SCALARS] + [WHOLE] * 7,
        out_specs=(WHOLE,) * 4,
        compiler_params=params(16),
        name="assemble",
    )(relay_target.reshape(-1), received, *operator, edges)
    from_right = shifted(to_left, -1)
    from_left = shifted(to_right, 1)

    basis, mapped, sums = pl.pallas_call(
        basis_kernel,
        out_shape=(pltpu.VMEM((4,) + field, F32), pltpu.VMEM((3,) + field, F32), pltpu.VMEM((6, values, rows), F32)),
        in_specs=[WHOLE] * 7,
        out_specs=(WHOLE,) * 3,
        scratch_shapes=[pltpu.VMEM((pairs, 2 * values, 2 * rows), BF16)],
        compiler_params=params(16),
        cost_estimate=cost(36 * blocks * unit, 32 * 2**20),
        name="basis",
    )(rhs, theta, *operator)

    basis_edge, mapped_edge, moments = pl.pallas_call(
        edge_kernel,
        out_shape=(
            pltpu.VMEM((3, 2 * EDGE, values, rows), F32),
            pltpu.VMEM((2, 2 * EDGE, values, rows), F32),
            jax.ShapeDtypeStruct((devices, 8, rows), F32),
        ),
        in_specs=[WHOLE] * 11,
        out_specs=(WHOLE,) * 3,
        compiler_params=params(16),
        name="edge",
    )(from_left, from_right, basis, mapped, sums, theta, *operator)
    gathered = lax.all_to_all(moments, AXES, split_axis=0, concat_axis=0, tiled=True)

    result = pl.BlockSpec((chunk, values, rows), lambda step: (step, 0, 0))
    return pl.pallas_call(
        combine_kernel,
        grid=(blocks // chunk,),
        out_shape=(jax.ShapeDtypeStruct(field, F32),) * 2,
        in_specs=[WHOLE] * 6,
        out_specs=(result, result),
        scratch_shapes=[pltpu.VMEM((7, values, rows), F32)],
        compiler_params=params(16),
        name="combine",
    )(gathered, theta, basis, mapped, basis_edge, mapped_edge)


def solution(mesh):
    placed = (
        P(AXES, None, None),
        P(AXES, None, None),
        P(AXES, None),
        P(AXES, None, None),
        P(AXES, None, None),
        P(AXES, None, None),
        P(AXES, None, None),
        P(AXES, None, None),
        P(AXES),
        P(AXES, None, None),
    )
    return jax.shard_map(
        body,
        mesh=mesh,
        in_specs=placed,
        out_specs=(P(AXES, None, None), P(AXES, None, None)),
        check_vma=False,
    )
```

```python
import functools

import jax
import jax.numpy as jnp
from jax import lax
from jax.experimental import pallas as pl
from jax.experimental.pallas import tpu as pltpu
from jax.sharding import PartitionSpec as P

AXES = ("dom", "sub")
EDGE = 3
EXTRA = 8
OCTAVE = 64.0
FULL = 32766.0
TINY = 1e-37
F32 = jnp.float32
BF16 = jnp.bfloat16
WHOLE = pl.BlockSpec(memory_space=pltpu.VMEM)
AWAY = pl.BlockSpec(memory_space=pl.ANY)
SCALARS = pl.BlockSpec(memory_space=pltpu.SMEM)


def params(mebibytes):
    return pltpu.CompilerParams(vmem_limit_bytes=mebibytes * 2**20)


def cost(flops, moved):
    return pl.CostEstimate(flops=int(flops), bytes_accessed=int(moved), transcendentals=0)


def layout(rows):
    def place(first, count):
        return slice(first * rows, (first + count) * rows)

    return (place(0, 1), place(1, 1)), place(2, 2), place(0, 2), place(2, 1), place(3, 1)


def dot(first, second):
    return jnp.dot(first, second, preferred_element_type=F32)


def parted(value):
    high = value.astype(BF16)
    return high, (value - high.astype(F32)).astype(BF16)


def tall(value):
    return jnp.concatenate(parted(value), axis=0)


def wide(value):
    return jnp.concatenate(parted(value), axis=1)


def by_wide(stacked, weights):
    rows, columns = stacked.shape[0] // 2, weights.shape[1] // 2
    out = dot(stacked, weights)
    return out[:rows, :columns] + (out[rows:, :columns] + out[:rows, columns:])


def by_pair(stacked, high, low):
    rows = stacked.shape[0] // 2
    out = dot(stacked, high)
    return out[:rows] + (out[rows:] + dot(stacked[:rows], low))


def pick_kernel(picks, counts, history, outgoing, *, slots):
    def step(entry, carry):
        live = (entry % slots) < counts[entry // slots]
        block = history[picks[entry]]
        outgoing[entry] = jnp.where(live, block, jnp.zeros_like(block))
        return carry

    total = outgoing.shape[0]
    lax.fori_loop(0, total, step, 0, unroll=8)


def prepare_kernel(coupling, diag, onward, precond, near, far, near_ends, far_ends, beside, trace, edges):
    step = pl.program_id(0)
    steps = pl.num_programs(0)
    blocks = diag.shape[0]
    rows = diag.shape[1]
    pre, high, low, cross, cross_t = layout(rows)
    total = jnp.zeros((rows, rows), F32)
    for local in range(blocks // 2):
        pair = step * (blocks // 2) + local
        for side in range(2):
            own = precond[2 * local + side]
            near[local, pre[side]] = wide(own)
            total = total + own * diag[2 * local + side]
        linked = onward[2 * local] * coupling[2 * pair].astype(F32)
        whole = jnp.concatenate(
            [
                jnp.concatenate([diag[2 * local], linked], axis=1),
                jnp.concatenate([linked.T, diag[2 * local + 1]], axis=1),
            ],
            axis=0,
        )
        near[local, high], far[local, low] = parted(whole)
        linked = onward[2 * local + 1] * coupling[2 * pair + 1].astype(F32)
        far[local, cross] = wide(linked)
        far[local, cross_t] = wide(linked.T)
    part = total.reshape(rows // 8, 8, rows).sum(axis=0)
    exact = functools.partial(jnp.dot, precision=lax.Precision.HIGHEST, preferred_element_type=F32)

    @pl.when(step == 0)
    def _():
        trace[...] = part
        near_ends[0] = near[0]
        far_ends[0] = far[0]
        beside[0] = near[1, pre[0]]
        first = precond[0]
        edges[2] = first
        edges[3] = exact(exact(first, diag[0]), first)

    @pl.when(step > 0)
    def _():
        trace[...] += part

    @pl.when(step == steps - 1)
    def _():
        near_ends[1] = near[blocks // 2 - 1]
        far_ends[1] = far[blocks // 2 - 1]
        beside[1] = near[blocks // 2 - 2, pre[1]]
        beside[2] = far[blocks // 2 - 2, cross]
        beside[3] = far[blocks // 2 - 2, cross_t]
        last = onward[blocks - 1] * coupling[steps * blocks - 1].astype(F32)
        mapped = exact(precond[blocks - 1], last)
        edges[0] = exact(last.T, mapped)
        edges[1] = exact(mapped.T, exact(diag[blocks - 1], mapped))


def mix_kernel(relay, arrived, mixing, trace, sending):
    total, values, rows = arrived.shape
    entries = trace.shape[0] * trace.shape[1]
    share = jnp.sum(jnp.sum(trace[...], axis=0, keepdims=True), axis=1, keepdims=True)
    share = jnp.maximum(jnp.broadcast_to(share, (1, rows)), TINY)
    share_code = jnp.floor(jnp.log2(share) * OCTAVE).astype(jnp.int32)
    lower = lax.broadcasted_iota(jnp.int32, (EXTRA, rows), 0) < EXTRA // 2

    def step(entry, carry):
        slot = relay[entry]
        tile = dot(arrived[slot], mixing[slot])
        peak = jnp.max(jnp.abs(tile), axis=0, keepdims=True)
        code = jnp.floor(jnp.log2(jnp.maximum(peak, TINY)) * OCTAVE) + 2.0
        scaled = tile * (FULL / jnp.exp2(code * (1.0 / OCTAVE)))
        scaled = jnp.clip(jnp.floor(scaled + 0.5), -32767.0, 32767.0)
        sending[entry, :values] = scaled.astype(jnp.int32).astype(jnp.int16)
        codes = jnp.where(lower, code.astype(jnp.int32), share_code)
        sending[entry, values:] = codes.astype(jnp.int16)
        return carry

    lax.fori_loop(0, total, step, 0, unroll=8)


def assemble_kernel(
    targets, received, near_ends, far_ends, beside, edges, near, rhs, theta_out, to_left, to_right, near_held, arrival, *, eigens
):
    total = received.shape[0]
    blocks, values, rows = rhs.shape
    copy = pltpu.make_async_copy(near, near_held, arrival)
    copy.start()
    rhs[...] = jnp.zeros_like(rhs)

    def step(entry, carry):
        extra = jnp.exp2(received[entry, values:].astype(jnp.int32).astype(F32) * (1.0 / OCTAVE))
        tile = received[entry, :values].astype(jnp.int32).astype(F32) * (extra[:1] * (1.0 / FULL))
        block = targets[entry]
        rhs[block] = rhs[block] + tile
        return carry + extra[EXTRA // 2 :]

    shares = lax.fori_loop(0, total, step, jnp.zeros((EXTRA // 2, rows), F32), unroll=8)
    theta = shares[:1] * (1.0 / eigens)
    theta_out[...] = jnp.broadcast_to(theta, theta_out.shape)

    weights, high, low, cross, cross_t = layout(rows)

    def pre(value, block):
        own = beside[block - 2] if block in (2, 3) else near_ends[block // 4, weights[block % 2]]
        return by_wide(tall(value), own)

    both = functools.partial(jnp.concatenate, axis=1)
    first = [rhs[block] for block in range(EDGE)]
    z0 = [pre(first[block], block) for block in range(EDGE)]
    q1 = by_pair(tall(both(z0[:2])), near_ends[0, high], far_ends[0, low]) - both([theta, theta]) * both(first[:2])
    q1 = [q1[:, :rows], q1[:, rows:] + by_wide(tall(z0[2]), far_ends[0, cross_t])]
    z1 = [pre(q1[block], block) for block in range(2)]
    q2 = by_pair(tall(both(z1)), near_ends[0, high], far_ends[0, low])[:, :rows] - theta * q1[0]
    to_left[0] = z0[0]
    to_left[1] = z1[0]
    to_left[2] = pre(q2, 0)
    last = [rhs[blocks - EDGE + block] for block in range(EDGE)]
    z0 = [pre(last[block], EDGE + block) for block in range(EDGE)]
    q1 = by_pair(tall(both(z0[1:])), near_ends[1, high], far_ends[1, low]) - both([theta, theta]) * both(last[1:])
    q1 = [q1[:, :rows] + by_wide(tall(z0[0]), beside[2]), q1[:, rows:]]
    z1 = [pre(q1[block], 4 + block) for block in range(2)]
    q2 = by_pair(tall(both(z1)), near_ends[1, high], far_ends[1, low])[:, rows:] - theta * q1[1]
    for place, value in enumerate((z0[2], z1[1], pre(q2, 5))):
        to_right[place] = by_wide(tall(value), far_ends[1, cross])
    for half in range(2):
        part = slice(half * values, (half + 1) * values)
        to_right[3 + half] = edges[0, part]
        to_right[5 + half] = edges[1, part]
        to_left[3 + half] = edges[2, part]
        to_left[5 + half] = edges[3, part]
    copy.wait()


def basis_kernel(rhs, theta_in, near, far, basis, mapped, sums, stacked):
    blocks, values, rows = rhs.shape
    pairs = blocks // 2
    theta = theta_in[:1]
    theta_pair = jnp.concatenate([theta, theta], axis=1)
    weights, high, low, cross, cross_t = layout(rows)
    basis[0] = rhs[...]

    for level in range(3):
        even = jnp.zeros((values, rows), F32)
        for block in range(blocks):
            value = basis[level, block]
            image = by_wide(tall(value), near[block // 2, weights[block % 2]])
            mapped[level, block] = image
            image_high, image_low = parted(image)
            side = slice((block % 2) * rows, (block % 2 + 1) * rows)
            stacked[block // 2, :values, side] = image_high
            stacked[block // 2, values:, side] = image_low
            if EDGE <= block < blocks - EDGE:
                even = even + value * image
        sums[2 * level] = even
        odd = jnp.zeros((values, rows), F32)
        for pair in range(pairs):
            image = by_pair(stacked[pair], near[pair, high], far[pair, low])
            sides = [image[:, :rows], image[:, rows:]]
            if pair > 0:
                sides[0] = sides[0] + by_wide(stacked[pair - 1, :, rows:], far[pair - 1, cross])
            if pair < pairs - 1:
                sides[1] = sides[1] + by_wide(stacked[pair + 1, :, :rows], far[pair, cross_t])
            for side in range(2):
                block = 2 * pair + side
                value = sides[side] - theta * basis[level, block]
                basis[level + 1, block] = value
                if EDGE <= block < blocks - EDGE:
                    odd = odd + value * mapped[level, block]
        sums[2 * level + 1] = odd


def edge_kernel(
    from_left, from_right, basis, mapped, sums, theta_in, near_ends, far_ends, beside, basis_edge, mapped_edge, moments
):
    _, blocks, values, rows = basis.shape
    theta = theta_in[:1]

    weights, high, low, cross, cross_t = layout(rows)

    def pre(value, block):
        return by_wide(tall(value), near_ends[block // 4, weights[block % 2]])

    def pair_image(first, second, pair):
        out = by_pair(tall(jnp.concatenate([first, second], axis=1)), near_ends[pair, high], far_ends[pair, low])
        return out[:, :rows], out[:, rows:]

    def square(ref, place):
        return jnp.concatenate([ref[place], ref[place + 1]], axis=0)

    none = jnp.zeros((values, rows), F32)

    mirror = square(from_left, 3)
    second = square(from_left, 5) - theta * mirror
    mirror, second = wide(mirror), wide(second)
    start = tall(mapped[0, 0])
    dq1 = from_left[0]
    dz1 = pre(dq1, 0)
    z1 = mapped[1, 0] + dz1
    own, after = pair_image(dz1, none, 0)
    dq2 = (own - theta * dq1 + from_left[1] + by_wide(start, mirror), after)
    dz2 = (pre(dq2[0], 0), pre(dq2[1], 1))
    own, after = pair_image(dz2[0], dz2[1], 0)
    dq3 = (
        own - theta * dq2[0] + from_left[2] + by_wide(start, second) + by_wide(tall(z1), mirror),
        after - theta * dq2[1],
        by_wide(tall(dz2[1]), far_ends[0, cross]),
    )
    changes = [((0, dq1),), ((0, dq2[0]), (1, dq2[1])), ((0, dq3[0]), (1, dq3[1]), (2, dq3[2]))]
    images = [((0, dz1),), ((0, dz2[0]), (1, dz2[1]))]

    last = blocks - 1
    mirror = square(from_right, 3)
    second = square(from_right, 5) - theta * mirror
    mirror, second = wide(mirror), wide(second)
    start = tall(by_wide(tall(mapped[0, last]), far_ends[1, cross]))
    dq1 = by_wide(tall(from_right[0]), far_ends[1, cross_t])
    dz1 = pre(dq1, 5)
    z1 = mapped[1, last] + dz1
    before, own = pair_image(none, dz1, 1)
    ahead = from_right[1] + by_wide(start, mirror)
    dq2 = (own - theta * dq1 + by_wide(tall(ahead), far_ends[1, cross_t]), before)
    dz2 = (pre(dq2[0], 5), pre(dq2[1], 4))
    before, own = pair_image(dz2[1], dz2[0], 1)
    ahead = from_right[2] + by_wide(start, second) + by_wide(tall(by_wide(tall(z1), far_ends[1, cross])), mirror)
    dq3 = (
        own - theta * dq2[0] + by_wide(tall(ahead), far_ends[1, cross_t]),
        before - theta * dq2[1],
        by_wide(tall(dz2[1]), beside[3]),
    )
    changes[0] += ((5, dq1),)
    changes[1] += ((5, dq2[0]), (4, dq2[1]))
    changes[2] += ((5, dq3[0]), (4, dq3[1]), (3, dq3[2]))
    images[0] += ((5, dz1),)
    images[1] += ((5, dz2[0]), (4, dz2[1]))

    places = [0, 1, 2, blocks - 3, blocks - 2, blocks - 1]
    before = [rhs_block for rhs_block in (basis[0, block] for block in places)]
    lane = lax.broadcasted_iota(jnp.int32, (values, rows), 1)
    table = none
    for level in range(3):
        image = [mapped[level, block] for block in places]
        if level > 0:
            for place, change in images[level - 1]:
                image[place] = image[place] + change
            for place in range(2 * EDGE):
                mapped_edge[level - 1, place] = image[place]
        now = [basis[level + 1, block] for block in places]
        for place, change in changes[level]:
            now[place] = now[place] + change
        even = sums[2 * level]
        odd = sums[2 * level + 1]
        for place in range(2 * EDGE):
            basis_edge[level, place] = now[place]
            even = even + before[place] * image[place]
            odd = odd + now[place] * image[place]
        table = jnp.where(lane == 2 * level, jnp.sum(even, axis=1, keepdims=True), table)
        table = jnp.where(lane == 2 * level + 1, jnp.sum(odd, axis=1, keepdims=True), table)
        before = now
    flipped = jnp.concatenate([table, jnp.zeros((rows - values, rows), F32)], axis=0).T[:8]
    for peer in range(moments.shape[0]):
        moments[peer] = flipped


def combine_kernel(moments, theta_in, basis, mapped, basis_edge, mapped_edge, solution, residual, factors):
    step = pl.program_id(0)
    _, blocks, values, rows = basis.shape
    chunk = solution.shape[0]

    @pl.when(step == 0)
    def _():
        total = jnp.sum(moments[...], axis=0)
        theta = theta_in[:1]
        m0, m1, m2, m3, m4, m5 = (total[place : place + 1] for place in range(6))
        m0 = m0 + TINY
        l10 = m1 / m0
        l20 = m2 / m0
        d1 = m2 - l10 * m1 + TINY
        g21 = m3 - l20 * m1
        l21 = g21 / d1
        d2 = m4 - l20 * m2 - l21 * g21 + TINY
        b1 = l10 * m3 - m4
        b2 = l20 * m3 - l21 * b1 - m5
        c2 = b2 / d2
        c1 = b1 / d1 - l21 * c2
        c0 = -m3 / m0 - l10 * c1 - l20 * c2
        scale = 1.0 / (c0 - theta * (c1 - theta * (c2 - theta)))
        c0, c1, c2, c3 = c0 * scale, c1 * scale, c2 * scale, scale
        y2 = -c3
        y1 = -c2 - theta * y2
        y0 = -c1 - theta * y1
        table = jnp.concatenate([c0, c1, c2, c3, y0, y1, y2, jnp.zeros((rows - 7, rows), F32)], axis=0).T
        for place in range(7):
            factors[place] = jnp.broadcast_to(table[:values, place : place + 1], (values, rows))

    factor = [factors[place] for place in range(7)]

    def store(place, q, z):
        residual[place] = (q[0] * factor[0] + q[1] * factor[1]) + (q[2] * factor[2] + q[3] * factor[3])
        solution[place] = z[0] * factor[4] + z[1] * factor[5] + z[2] * factor[6]

    for place in range(chunk):
        block = step * chunk + place
        store(place, [basis[level, block] for level in range(4)], [mapped[level, block] for level in range(3)])

    def edge(place, block, entry):
        q = [basis[0, block]] + [basis_edge[level, entry] for level in range(3)]
        z = [mapped[0, block]] + [mapped_edge[level, entry] for level in range(2)]
        store(place, q, z)

    @pl.when(step == 0)
    def _():
        for entry in range(EDGE):
            edge(entry, entry, entry)

    @pl.when(step == pl.num_programs(0) - 1)
    def _():
        for entry in range(EDGE):
            edge(chunk - EDGE + entry, blocks - EDGE + entry, EDGE + entry)


def shifted(value, steps):
    count = lax.axis_size(AXES)
    first, last = (max(0, -steps), min(count, count - steps))
    return lax.ppermute(value, AXES, [(source, source + steps) for source in range(first, last)])


def body(
    history,
    send_list,
    send_count,
    mixed_mass,
    relay_list,
    relay_target,
    mass_diag,
    mass_next,
    coupling,
    precond,
):
    devices = lax.axis_size(AXES)
    slots = send_list.shape[2]
    total = devices * slots
    values, rows = history.shape[1:]
    blocks = mass_diag.shape[0]
    pairs = blocks // 2
    field = (blocks, values, rows)
    stay = functools.partial(pltpu.with_memory_space_constraint, memory_space=pltpu.HBM)
    unit = 2 * values * rows * rows

    outgoing = pl.pallas_call(
        functools.partial(pick_kernel, slots=slots),
        out_shape=jax.ShapeDtypeStruct((total, values, rows), BF16),
        in_specs=[SCALARS, SCALARS, WHOLE],
        out_specs=WHOLE,
        compiler_params=params(10),
        name="pick",
    )(stay(send_list.reshape(-1)), stay(send_count.reshape(-1)), stay(history))
    arrived = lax.all_to_all(outgoing, AXES, split_axis=0, concat_axis=0, tiled=True)

    chunk = 8
    matrix = pl.BlockSpec((chunk, rows, rows), lambda step: (step, 0, 0))
    half = (4 * rows, 2 * rows)
    near, far, *ends, trace, edges = pl.pallas_call(
        prepare_kernel,
        grid=(blocks // chunk,),
        out_shape=(
            pltpu.HBM((pairs,) + half, BF16),
            pltpu.HBM((pairs,) + half, BF16),
            pltpu.VMEM((2,) + half, BF16),
            pltpu.VMEM((2,) + half, BF16),
            pltpu.VMEM((4, rows, 2 * rows), BF16),
            pltpu.VMEM((8, rows), F32),
            pltpu.VMEM((4, rows, rows), F32),
        ),
        in_specs=[SCALARS, matrix, matrix, matrix],
        out_specs=(pl.BlockSpec((chunk // 2,) + half, lambda step: (step, 0, 0)),) * 2 + (WHOLE,) * 5,
        compiler_params=params(16),
        cost_estimate=cost(0, 28 * 2**20),
        name="prepare",
    )(coupling, stay(mass_diag), stay(mass_next), stay(precond))

    sending = pl.pallas_call(
        mix_kernel,
        out_shape=jax.ShapeDtypeStruct((total, values + EXTRA, rows), jnp.int16),
        in_specs=[SCALARS, WHOLE, WHOLE, WHOLE],
        out_specs=WHOLE,
        compiler_params=params(10),
        name="mix",
    )(relay_list.reshape(-1), arrived, mixed_mass, trace)
    received = lax.all_to_all(sending, AXES, split_axis=0, concat_axis=0, tiled=True)

    packet = jax.ShapeDtypeStruct((EDGE + 4, values, rows), F32)
    rhs, theta, to_left, to_right, near_held = pl.pallas_call(
        functools.partial(assemble_kernel, eigens=devices * blocks * rows),
        out_shape=(pltpu.VMEM(field, F32), pltpu.VMEM((8, rows), F32), packet, packet, pltpu.VMEM((pairs,) + half, BF16)),
        in_specs=[SCALARS] + [WHOLE] * 5 + [AWAY],
        out_specs=(WHOLE,) * 5,
        scratch_shapes=[pltpu.SemaphoreType.DMA],
        compiler_params=params(10),
        name="assemble",
    )(relay_target.reshape(-1), received, *ends, edges, stay(near))
    from_right = shifted(to_left, -1)
    from_left = shifted(to_right, 1)

    basis, mapped, sums = pl.pallas_call(
        basis_kernel,
        out_shape=(pltpu.VMEM((4,) + field, F32), pltpu.VMEM((3,) + field, F32), pltpu.VMEM((6, values, rows), F32)),
        in_specs=[WHOLE] * 4,
        out_specs=(WHOLE,) * 3,
        scratch_shapes=[pltpu.VMEM((pairs, 2 * values, 2 * rows), BF16)],
        compiler_params=params(10),
        cost_estimate=cost(36 * blocks * unit, 32 * 2**20),
        name="basis",
    )(rhs, theta, near_held, far)

    basis_edge, mapped_edge, moments = pl.pallas_call(
        edge_kernel,
        out_shape=(
            pltpu.VMEM((3, 2 * EDGE, values, rows), F32),
            pltpu.VMEM((2, 2 * EDGE, values, rows), F32),
            jax.ShapeDtypeStruct((devices, 8, rows), F32),
        ),
        in_specs=[WHOLE] * 9,
        out_specs=(WHOLE,) * 3,
        compiler_params=params(10),
        name="edge",
    )(from_left, from_right, basis, mapped, sums, theta, *ends)
    gathered = lax.all_to_all(moments, AXES, split_axis=0, concat_axis=0, tiled=True)

    result = pl.BlockSpec((chunk, values, rows), lambda step: (step, 0, 0))
    return pl.pallas_call(
        combine_kernel,
        grid=(blocks // chunk,),
        out_shape=(jax.ShapeDtypeStruct(field, F32),) * 2,
        in_specs=[WHOLE] * 6,
        out_specs=(result, result),
        scratch_shapes=[pltpu.VMEM((7, values, rows), F32)],
        compiler_params=params(10),
        name="combine",
    )(gathered, theta, basis, mapped, basis_edge, mapped_edge)


def solution(mesh):
    placed = (
        P(AXES, None, None),
        P(AXES, None, None),
        P(AXES, None),
        P(AXES, None, None),
        P(AXES, None, None),
        P(AXES, None, None),
        P(AXES, None, None),
        P(AXES, None, None),
        P(AXES),
        P(AXES, None, None),
    )
    return jax.shard_map(
        body,
        mesh=mesh,
        in_specs=placed,
        out_specs=(P(AXES, None, None), P(AXES, None, None)),
        check_vma=False,
    )
```

```python
import functools

import jax
import jax.numpy as jnp
from jax import lax
from jax.experimental import pallas as pl
from jax.experimental.pallas import tpu as pltpu
from jax.sharding import PartitionSpec as P

AXES = ("dom", "sub")
EDGE = 3
EXTRA = 8
OCTAVE = 64.0
FULL = 32766.0
TINY = 1e-37
F32 = jnp.float32
BF16 = jnp.bfloat16
WHOLE = pl.BlockSpec(memory_space=pltpu.VMEM)
AWAY = pl.BlockSpec(memory_space=pl.ANY)
SCALARS = pl.BlockSpec(memory_space=pltpu.SMEM)


def params(mebibytes):
    return pltpu.CompilerParams(vmem_limit_bytes=mebibytes * 2**20)


def cost(flops, moved):
    return pl.CostEstimate(flops=int(flops), bytes_accessed=int(moved), transcendentals=0)


def layout(rows):
    def place(first, count):
        return slice(first * rows, (first + count) * rows)

    return (place(0, 1), place(1, 1)), place(0, 2), place(2, 2), place(0, 1), place(1, 1)


def dot(first, second):
    return jnp.dot(first, second, preferred_element_type=F32)


def parted(value):
    high = value.astype(BF16)
    return high, (value - high.astype(F32)).astype(BF16)


def tall(value):
    return jnp.concatenate(parted(value), axis=0)


def wide(value):
    return jnp.concatenate(parted(value), axis=1)


def by_wide(stacked, weights):
    rows, columns = stacked.shape[0] // 2, weights.shape[1] // 2
    out = dot(stacked, weights)
    return out[:rows, :columns] + (out[rows:, :columns] + out[:rows, columns:])


def by_pair(stacked, high, low):
    rows = stacked.shape[0] // 2
    out = dot(stacked, high)
    return out[:rows] + (out[rows:] + dot(stacked[:rows], low))


def pick_kernel(picks, counts, history, outgoing, *, slots):
    def step(entry, carry):
        live = (entry % slots) < counts[entry // slots]
        block = history[picks[entry]]
        outgoing[entry] = jnp.where(live, block, jnp.zeros_like(block))
        return carry

    total = outgoing.shape[0]
    lax.fori_loop(0, total, step, 0, unroll=8)


def prepare_kernel(coupling, diag, onward, precond, pre, mass, link, pre_ends, mass_ends, link_ends, beside, trace, edges):
    step = pl.program_id(0)
    steps = pl.num_programs(0)
    blocks = diag.shape[0]
    rows = diag.shape[1]
    sides, high, low, plain, turned = layout(rows)
    total = jnp.zeros((rows, rows), F32)
    for local in range(blocks // 2):
        pair = step * (blocks // 2) + local
        for side in range(2):
            own = precond[2 * local + side]
            pre[local, sides[side]] = wide(own)
            total = total + own * diag[2 * local + side]
        linked = onward[2 * local] * coupling[2 * pair].astype(F32)
        whole = jnp.concatenate(
            [
                jnp.concatenate([diag[2 * local], linked], axis=1),
                jnp.concatenate([linked.T, diag[2 * local + 1]], axis=1),
            ],
            axis=0,
        )
        mass[local, high], mass[local, low] = parted(whole)
        linked = onward[2 * local + 1] * coupling[2 * pair + 1].astype(F32)
        link[local, plain] = wide(linked)
        link[local, turned] = wide(linked.T)
    part = total.reshape(rows // 8, 8, rows).sum(axis=0)
    exact = functools.partial(jnp.dot, precision=lax.Precision.HIGHEST, preferred_element_type=F32)

    @pl.when(step == 0)
    def _():
        trace[...] = part
        pre_ends[0] = pre[0]
        mass_ends[0] = mass[0]
        link_ends[0] = link[0]
        beside[0] = pre[1, sides[0]]
        first = precond[0]
        edges[2] = first
        edges[3] = exact(exact(first, diag[0]), first)

    @pl.when(step > 0)
    def _():
        trace[...] += part

    @pl.when(step == steps - 1)
    def _():
        pre_ends[1] = pre[blocks // 2 - 1]
        mass_ends[1] = mass[blocks // 2 - 1]
        link_ends[1] = link[blocks // 2 - 1]
        beside[1] = pre[blocks // 2 - 2, sides[1]]
        beside[2] = link[blocks // 2 - 2, plain]
        beside[3] = link[blocks // 2 - 2, turned]
        last = onward[blocks - 1] * coupling[steps * blocks - 1].astype(F32)
        mapped = exact(precond[blocks - 1], last)
        edges[0] = exact(last.T, mapped)
        edges[1] = exact(mapped.T, exact(diag[blocks - 1], mapped))


def mix_kernel(relay, arrived, mixing, trace, sending):
    total, values, rows = arrived.shape
    entries = trace.shape[0] * trace.shape[1]
    share = jnp.sum(jnp.sum(trace[...], axis=0, keepdims=True), axis=1, keepdims=True)
    share = jnp.maximum(jnp.broadcast_to(share, (1, rows)), TINY)
    share_code = jnp.floor(jnp.log2(share) * OCTAVE).astype(jnp.int32)
    lower = lax.broadcasted_iota(jnp.int32, (EXTRA, rows), 0) < EXTRA // 2

    def step(entry, carry):
        slot = relay[entry]
        tile = dot(arrived[slot], mixing[slot])
        peak = jnp.max(jnp.abs(tile), axis=0, keepdims=True)
        code = jnp.floor(jnp.log2(jnp.maximum(peak, TINY)) * OCTAVE) + 2.0
        scaled = tile * (FULL / jnp.exp2(code * (1.0 / OCTAVE)))
        scaled = jnp.clip(jnp.floor(scaled + 0.5), -32767.0, 32767.0)
        sending[entry, :values] = scaled.astype(jnp.int32).astype(jnp.int16)
        codes = jnp.where(lower, code.astype(jnp.int32), share_code)
        sending[entry, values:] = codes.astype(jnp.int16)
        return carry

    lax.fori_loop(0, total, step, 0, unroll=32)


def assemble_kernel(
    targets, received, pre_ends, mass_ends, link_ends, beside, edges, pre_away, rhs, theta_out, even_packet, odd_packet, pre, arrival, *, eigens
):
    total = received.shape[0]
    blocks, values, rows = rhs.shape
    copy = pltpu.make_async_copy(pre_away, pre, arrival)
    copy.start()
    rhs[...] = jnp.zeros_like(rhs)

    def step(entry, carry):
        extra = jnp.exp2(received[entry, values:].astype(jnp.int32).astype(F32) * (1.0 / OCTAVE))
        tile = received[entry, :values].astype(jnp.int32).astype(F32) * (extra[:1] * (1.0 / FULL))
        block = targets[entry]
        rhs[block] = rhs[block] + tile
        return carry + extra[EXTRA // 2 :]

    shares = lax.fori_loop(0, total, step, jnp.zeros((EXTRA // 2, rows), F32), unroll=8)
    theta = shares[:1] * (1.0 / eigens)
    theta_out[...] = jnp.broadcast_to(theta, theta_out.shape)

    sides, high, low, plain, turned = layout(rows)

    def conditioned(value, block):
        own = beside[block - 2] if block in (2, 3) else pre_ends[block // 4, sides[block % 2]]
        return by_wide(tall(value), own)

    both = functools.partial(jnp.concatenate, axis=1)
    first = [rhs[block] for block in range(EDGE)]
    z0 = [conditioned(first[block], block) for block in range(EDGE)]
    q1 = by_pair(tall(both(z0[:2])), mass_ends[0, high], mass_ends[0, low]) - both([theta, theta]) * both(first[:2])
    q1 = [q1[:, :rows], q1[:, rows:] + by_wide(tall(z0[2]), link_ends[0, turned])]
    z1 = [conditioned(q1[block], block) for block in range(2)]
    q2 = by_pair(tall(both(z1)), mass_ends[0, high], mass_ends[0, low])[:, :rows] - theta * q1[0]
    to_left = [z0[0], z1[0], conditioned(q2, 0)]
    last = [rhs[blocks - EDGE + block] for block in range(EDGE)]
    z0 = [conditioned(last[block], EDGE + block) for block in range(EDGE)]
    q1 = by_pair(tall(both(z0[1:])), mass_ends[1, high], mass_ends[1, low]) - both([theta, theta]) * both(last[1:])
    q1 = [q1[:, :rows] + by_wide(tall(z0[0]), beside[2]), q1[:, rows:]]
    z1 = [conditioned(q1[block], 4 + block) for block in range(2)]
    q2 = by_pair(tall(both(z1)), mass_ends[1, high], mass_ends[1, low])[:, rows:] - theta * q1[1]
    to_right = [by_wide(tall(value), link_ends[1, plain]) for value in (z0[2], z1[1], conditioned(q2, 5))]
    for product in range(4):
        for half in range(2):
            (to_right if product < 2 else to_left).append(edges[product, half * values : (half + 1) * values])
    even = stands_even()
    for entry in range(EDGE + 4):
        even_packet[entry] = jnp.where(even, to_right[entry], to_left[entry])
        odd_packet[entry] = jnp.where(even, to_left[entry], to_right[entry])
    copy.wait()


def basis_kernel(rhs, theta_in, pre, mass, link_away, basis, mapped, sums, stacked, link, arrival):
    blocks, values, rows = rhs.shape
    pairs = blocks // 2
    theta = theta_in[:1]
    theta_pair = jnp.concatenate([theta, theta], axis=1)
    sides, high, low, plain, turned = layout(rows)
    copy = pltpu.make_async_copy(link_away, link, arrival)
    copy.start()
    basis[0] = rhs[...]

    for level in range(3):
        even = jnp.zeros((values, rows), F32)
        for block in range(blocks):
            value = basis[level, block]
            image = by_wide(tall(value), pre[block // 2, sides[block % 2]])
            mapped[level, block] = image
            image_high, image_low = parted(image)
            side = slice((block % 2) * rows, (block % 2 + 1) * rows)
            stacked[block // 2, :values, side] = image_high
            stacked[block // 2, values:, side] = image_low
            if EDGE <= block < blocks - EDGE:
                even = even + value * image
        sums[2 * level] = even
        if level == 0:
            copy.wait()
        odd = jnp.zeros((values, rows), F32)
        for pair in range(pairs):
            image = by_pair(stacked[pair], mass[pair, high], mass[pair, low])
            parts = [image[:, :rows], image[:, rows:]]
            if pair > 0:
                parts[0] = parts[0] + by_wide(stacked[pair - 1, :, rows:], link[pair - 1, plain])
            if pair < pairs - 1:
                parts[1] = parts[1] + by_wide(stacked[pair + 1, :, :rows], link[pair, turned])
            for side in range(2):
                block = 2 * pair + side
                value = parts[side] - theta * basis[level, block]
                basis[level + 1, block] = value
                if EDGE <= block < blocks - EDGE:
                    odd = odd + value * mapped[level, block]
        sums[2 * level + 1] = odd


def edge_kernel(
    even_met, odd_met, basis, mapped, sums, theta_in, pre_ends, mass_ends, link_ends, beside, basis_edge, mapped_edge, moments
):
    _, blocks, values, rows = basis.shape
    theta = theta_in[:1]
    even = stands_even()
    from_left = [jnp.where(even, odd_met[entry], even_met[entry]) for entry in range(EDGE + 4)]
    from_right = [jnp.where(even, even_met[entry], odd_met[entry]) for entry in range(EDGE + 4)]

    sides, high, low, plain, turned = layout(rows)

    def conditioned(value, block):
        return by_wide(tall(value), pre_ends[block // 4, sides[block % 2]])

    def pair_image(first, second, pair):
        out = by_pair(tall(jnp.concatenate([first, second], axis=1)), mass_ends[pair, high], mass_ends[pair, low])
        return out[:, :rows], out[:, rows:]

    def square(ref, place):
        return jnp.concatenate([ref[place], ref[place + 1]], axis=0)

    none = jnp.zeros((values, rows), F32)

    mirror = square(from_left, 3)
    second = square(from_left, 5) - theta * mirror
    mirror, second = wide(mirror), wide(second)
    start = tall(mapped[0, 0])
    dq1 = from_left[0]
    dz1 = conditioned(dq1, 0)
    z1 = mapped[1, 0] + dz1
    own, after = pair_image(dz1, none, 0)
    dq2 = (own - theta * dq1 + from_left[1] + by_wide(start, mirror), after)
    dz2 = (conditioned(dq2[0], 0), conditioned(dq2[1], 1))
    own, after = pair_image(dz2[0], dz2[1], 0)
    dq3 = (
        own - theta * dq2[0] + from_left[2] + by_wide(start, second) + by_wide(tall(z1), mirror),
        after - theta * dq2[1],
        by_wide(tall(dz2[1]), link_ends[0, plain]),
    )
    changes = [((0, dq1),), ((0, dq2[0]), (1, dq2[1])), ((0, dq3[0]), (1, dq3[1]), (2, dq3[2]))]
    images = [((0, dz1),), ((0, dz2[0]), (1, dz2[1]))]

    last = blocks - 1
    mirror = square(from_right, 3)
    second = square(from_right, 5) - theta * mirror
    mirror, second = wide(mirror), wide(second)
    start = tall(by_wide(tall(mapped[0, last]), link_ends[1, plain]))
    dq1 = by_wide(tall(from_right[0]), link_ends[1, turned])
    dz1 = conditioned(dq1, 5)
    z1 = mapped[1, last] + dz1
    before, own = pair_image(none, dz1, 1)
    ahead = from_right[1] + by_wide(start, mirror)
    dq2 = (own - theta * dq1 + by_wide(tall(ahead), link_ends[1, turned]), before)
    dz2 = (conditioned(dq2[0], 5), conditioned(dq2[1], 4))
    before, own = pair_image(dz2[1], dz2[0], 1)
    ahead = from_right[2] + by_wide(start, second) + by_wide(tall(by_wide(tall(z1), link_ends[1, plain])), mirror)
    dq3 = (
        own - theta * dq2[0] + by_wide(tall(ahead), link_ends[1, turned]),
        before - theta * dq2[1],
        by_wide(tall(dz2[1]), beside[3]),
    )
    changes[0] += ((5, dq1),)
    changes[1] += ((5, dq2[0]), (4, dq2[1]))
    changes[2] += ((5, dq3[0]), (4, dq3[1]), (3, dq3[2]))
    images[0] += ((5, dz1),)
    images[1] += ((5, dz2[0]), (4, dz2[1]))

    places = [0, 1, 2, blocks - 3, blocks - 2, blocks - 1]
    before = [rhs_block for rhs_block in (basis[0, block] for block in places)]
    lane = lax.broadcasted_iota(jnp.int32, (values, rows), 1)
    table = none
    for level in range(3):
        image = [mapped[level, block] for block in places]
        if level > 0:
            for spot, change in images[level - 1]:
                image[spot] = image[spot] + change
            for spot in range(2 * EDGE):
                mapped_edge[level - 1, spot] = image[spot]
        now = [basis[level + 1, block] for block in places]
        for spot, change in changes[level]:
            now[spot] = now[spot] + change
        even = sums[2 * level]
        odd = sums[2 * level + 1]
        for spot in range(2 * EDGE):
            basis_edge[level, spot] = now[spot]
            even = even + before[spot] * image[spot]
            odd = odd + now[spot] * image[spot]
        table = jnp.where(lane == 2 * level, jnp.sum(even, axis=1, keepdims=True), table)
        table = jnp.where(lane == 2 * level + 1, jnp.sum(odd, axis=1, keepdims=True), table)
        before = now
    flipped = jnp.concatenate([table, jnp.zeros((rows - values, rows), F32)], axis=0).T[:8]
    for peer in range(moments.shape[0]):
        moments[peer] = flipped


def combine_kernel(moments, theta_in, basis, mapped, basis_edge, mapped_edge, solution, residual, factors):
    step = pl.program_id(0)
    _, blocks, values, rows = basis.shape
    chunk = solution.shape[0]

    @pl.when(step == 0)
    def _():
        total = jnp.sum(moments[...], axis=0)
        theta = theta_in[:1]
        m0, m1, m2, m3, m4, m5 = (total[place : place + 1] for place in range(6))
        m0 = m0 + TINY
        l10 = m1 / m0
        l20 = m2 / m0
        d1 = m2 - l10 * m1 + TINY
        g21 = m3 - l20 * m1
        l21 = g21 / d1
        d2 = m4 - l20 * m2 - l21 * g21 + TINY
        b1 = l10 * m3 - m4
        b2 = l20 * m3 - l21 * b1 - m5
        c2 = b2 / d2
        c1 = b1 / d1 - l21 * c2
        c0 = -m3 / m0 - l10 * c1 - l20 * c2
        scale = 1.0 / (c0 - theta * (c1 - theta * (c2 - theta)))
        c0, c1, c2, c3 = c0 * scale, c1 * scale, c2 * scale, scale
        y2 = -c3
        y1 = -c2 - theta * y2
        y0 = -c1 - theta * y1
        table = jnp.concatenate([c0, c1, c2, c3, y0, y1, y2, jnp.zeros((rows - 7, rows), F32)], axis=0).T
        for place in range(7):
            factors[place] = jnp.broadcast_to(table[:values, place : place + 1], (values, rows))

    def store(first, count, basis_of, mapped_of):
        for row in range(0, values, 8):
            part = slice(row, row + 8)
            factor = [factors[place, part] for place in range(7)]
            for place in range(first, first + count):
                q = basis_of(place, part)
                z = mapped_of(place, part)
                residual[place, part] = (q[0] * factor[0] + q[1] * factor[1]) + (q[2] * factor[2] + q[3] * factor[3])
                solution[place, part] = z[0] * factor[4] + z[1] * factor[5] + z[2] * factor[6]

    store(
        0,
        chunk,
        lambda place, part: [basis[level, step * chunk + place, part] for level in range(4)],
        lambda place, part: [mapped[level, step * chunk + place, part] for level in range(3)],
    )

    def edge(first, block, entry):
        store(
            first,
            EDGE,
            lambda place, part: [basis[0, block - first + place, part]]
            + [basis_edge[level, entry - first + place, part] for level in range(3)],
            lambda place, part: [mapped[0, block - first + place, part]]
            + [mapped_edge[level, entry - first + place, part] for level in range(2)],
        )

    @pl.when(step == 0)
    def _():
        edge(0, 0, 0)

    @pl.when(step == pl.num_programs(0) - 1)
    def _():
        edge(chunk - EDGE, blocks - EDGE, EDGE)


def stands_even():
    return (lax.axis_index(AXES[0]) * lax.axis_size(AXES[1]) + lax.axis_index(AXES[1])) % 2 == 0


def exchanged(value, first):
    swaps = [(one, one + 1) for one in range(first, lax.axis_size(AXES) - 1, 2)]
    return lax.ppermute(value, AXES, swaps + [(other, one) for one, other in swaps])


def body(
    history,
    send_list,
    send_count,
    mixed_mass,
    relay_list,
    relay_target,
    mass_diag,
    mass_next,
    coupling,
    precond,
):
    devices = lax.axis_size(AXES)
    slots = send_list.shape[2]
    total = devices * slots
    values, rows = history.shape[1:]
    blocks = mass_diag.shape[0]
    pairs = blocks // 2
    field = (blocks, values, rows)
    stay = functools.partial(pltpu.with_memory_space_constraint, memory_space=pltpu.HBM)
    unit = 2 * values * rows * rows

    outgoing = pl.pallas_call(
        functools.partial(pick_kernel, slots=slots),
        out_shape=jax.ShapeDtypeStruct((total, values, rows), BF16),
        in_specs=[SCALARS, SCALARS, WHOLE],
        out_specs=WHOLE,
        compiler_params=params(10),
        name="pick",
    )(stay(send_list.reshape(-1)), stay(send_count.reshape(-1)), stay(history))
    arrived = lax.all_to_all(outgoing, AXES, split_axis=0, concat_axis=0, tiled=True)

    chunk = 16
    matrix = pl.BlockSpec((chunk, rows, rows), lambda step: (step, 0, 0))
    pre_part = link_part = (2 * rows, 2 * rows)
    mass_part = (4 * rows, 2 * rows)
    pre, mass, link, *ends, trace, edges = pl.pallas_call(
        prepare_kernel,
        grid=(blocks // chunk,),
        out_shape=(
            *(pltpu.HBM((pairs,) + part, BF16) for part in (pre_part, mass_part, link_part)),
            *(pltpu.VMEM((2,) + part, BF16) for part in (pre_part, mass_part, link_part)),
            pltpu.VMEM((4, rows, 2 * rows), BF16),
            pltpu.VMEM((8, rows), F32),
            pltpu.VMEM((4, rows, rows), F32),
        ),
        in_specs=[SCALARS, matrix, matrix, matrix],
        out_specs=tuple(
            pl.BlockSpec((chunk // 2,) + part, lambda step: (step, 0, 0)) for part in (pre_part, mass_part, link_part)
        )
        + (WHOLE,) * 6,
        compiler_params=params(28),
        cost_estimate=cost(0, 28 * 2**20),
        name="prepare",
    )(stay(coupling), stay(mass_diag), stay(mass_next), stay(precond))

    sending = pl.pallas_call(
        mix_kernel,
        out_shape=jax.ShapeDtypeStruct((total, values + EXTRA, rows), jnp.int16),
        in_specs=[SCALARS, WHOLE, WHOLE, WHOLE],
        out_specs=WHOLE,
        compiler_params=params(10),
        name="mix",
    )(relay_list.reshape(-1), arrived, mixed_mass, trace)
    received = lax.all_to_all(sending, AXES, split_axis=0, concat_axis=0, tiled=True)

    packet = jax.ShapeDtypeStruct((EDGE + 4, values, rows), F32)
    rhs, theta, even_packet, odd_packet, pre_held = pl.pallas_call(
        functools.partial(assemble_kernel, eigens=devices * blocks * rows),
        out_shape=(pltpu.VMEM(field, F32), pltpu.VMEM((8, rows), F32), packet, packet, pltpu.VMEM((pairs,) + pre_part, BF16)),
        in_specs=[SCALARS] + [WHOLE] * 6 + [AWAY],
        out_specs=(WHOLE,) * 5,
        scratch_shapes=[pltpu.SemaphoreType.DMA],
        compiler_params=params(10),
        name="assemble",
    )(relay_target.reshape(-1), received, *ends, edges, stay(pre))
    even_met = exchanged(even_packet, 0)
    odd_met = exchanged(odd_packet, 1)

    basis, mapped, sums = pl.pallas_call(
        basis_kernel,
        out_shape=(pltpu.VMEM((4,) + field, F32), pltpu.VMEM((3,) + field, F32), pltpu.VMEM((6, values, rows), F32)),
        in_specs=[WHOLE] * 4 + [AWAY],
        out_specs=(WHOLE,) * 3,
        scratch_shapes=[
            pltpu.VMEM((pairs, 2 * values, 2 * rows), BF16),
            pltpu.VMEM((pairs,) + link_part, BF16),
            pltpu.SemaphoreType.DMA,
        ],
        compiler_params=params(12),
        cost_estimate=cost(36 * blocks * unit, 32 * 2**20),
        name="basis",
    )(rhs, theta, pre_held, mass, stay(link))

    basis_edge, mapped_edge, moments = pl.pallas_call(
        edge_kernel,
        out_shape=(
            pltpu.VMEM((3, 2 * EDGE, values, rows), F32),
            pltpu.VMEM((2, 2 * EDGE, values, rows), F32),
            jax.ShapeDtypeStruct((devices, 8, rows), F32),
        ),
        in_specs=[WHOLE] * 10,
        out_specs=(WHOLE,) * 3,
        compiler_params=params(10),
        name="edge",
    )(even_met, odd_met, basis, mapped, sums, theta, *ends)
    gathered = lax.all_to_all(moments, AXES, split_axis=0, concat_axis=0, tiled=True)

    chunk = 16
    result = pl.BlockSpec((chunk, values, rows), lambda step: (step, 0, 0))
    return pl.pallas_call(
        combine_kernel,
        grid=(blocks // chunk,),
        out_shape=(jax.ShapeDtypeStruct(field, F32),) * 2,
        in_specs=[WHOLE] * 6,
        out_specs=(result, result),
        scratch_shapes=[pltpu.VMEM((7, values, rows), F32)],
        compiler_params=params(10),
        name="combine",
    )(gathered, theta, basis, mapped, basis_edge, mapped_edge)


def solution(mesh):
    placed = (
        P(AXES, None, None),
        P(AXES, None, None),
        P(AXES, None),
        P(AXES, None, None),
        P(AXES, None, None),
        P(AXES, None, None),
        P(AXES, None, None),
        P(AXES, None, None),
        P(AXES),
        P(AXES, None, None),
    )
    return jax.shard_map(
        body,
        mesh=mesh,
        in_specs=placed,
        out_specs=(P(AXES, None, None), P(AXES, None, None)),
        check_vma=False,
    )
```

```python
import functools

import jax
import jax.numpy as jnp
from jax import lax
from jax.experimental import pallas as pl
from jax.experimental.pallas import tpu as pltpu
from jax.sharding import PartitionSpec as P

AXES = ("dom", "sub")
EDGE = 3
EXTRA = 8
OCTAVE = 64.0
FULL = 32766.0
TINY = 1e-37
F32 = jnp.float32
BF16 = jnp.bfloat16
WHOLE = pl.BlockSpec(memory_space=pltpu.VMEM)
AWAY = pl.BlockSpec(memory_space=pl.ANY)
SCALARS = pl.BlockSpec(memory_space=pltpu.SMEM)


def params(mebibytes):
    return pltpu.CompilerParams(vmem_limit_bytes=mebibytes * 2**20)


def cost(flops, moved):
    return pl.CostEstimate(flops=int(flops), bytes_accessed=int(moved), transcendentals=0)


def layout(rows):
    def place(first, count):
        return slice(first * rows, (first + count) * rows)

    return (place(0, 1), place(1, 1)), place(0, 2), place(2, 2), place(0, 1), place(1, 1)


def dot(first, second):
    return jnp.dot(first, second, preferred_element_type=F32)


def parted(value):
    high = value.astype(BF16)
    return high, (value - high.astype(F32)).astype(BF16)


def tall(value):
    return jnp.concatenate(parted(value), axis=0)


def wide(value):
    return jnp.concatenate(parted(value), axis=1)


def by_wide(stacked, weights):
    rows, columns = stacked.shape[0] // 2, weights.shape[1] // 2
    out = dot(stacked, weights)
    return out[:rows, :columns] + (out[rows:, :columns] + out[:rows, columns:])


def by_pair(stacked, high, low):
    rows = stacked.shape[0] // 2
    out = dot(stacked, high)
    return out[:rows] + (out[rows:] + dot(stacked[:rows], low))


def pick_kernel(picks, counts, history, outgoing, *, slots):
    def step(entry, carry):
        live = (entry % slots) < counts[entry // slots]
        block = history[picks[entry]]
        outgoing[entry] = jnp.where(live, block, jnp.zeros_like(block))
        return carry

    total = outgoing.shape[0]
    lax.fori_loop(0, total, step, 0, unroll=8)


def prepare_kernel(coupling, diag, onward, precond, pre, mass, link, pre_ends, mass_ends, link_ends, beside, trace, edges):
    step = pl.program_id(0)
    steps = pl.num_programs(0)
    blocks = diag.shape[0]
    rows = diag.shape[1]
    sides, high, low, plain, turned = layout(rows)
    total = jnp.zeros((rows, rows), F32)
    for local in range(blocks // 2):
        pair = step * (blocks // 2) + local
        for side in range(2):
            own = precond[2 * local + side]
            pre[local, sides[side]] = wide(own)
            total = total + own * diag[2 * local + side]
        linked = onward[2 * local] * coupling[2 * pair].astype(F32)
        whole = jnp.concatenate(
            [
                jnp.concatenate([diag[2 * local], linked], axis=1),
                jnp.concatenate([linked.T, diag[2 * local + 1]], axis=1),
            ],
            axis=0,
        )
        mass[local, high], mass[local, low] = parted(whole)
        linked = onward[2 * local + 1] * coupling[2 * pair + 1].astype(F32)
        link[local, plain] = wide(linked)
        link[local, turned] = wide(linked.T)
    part = total.reshape(rows // 8, 8, rows).sum(axis=0)
    exact = functools.partial(jnp.dot, precision=lax.Precision.HIGHEST, preferred_element_type=F32)

    @pl.when(step == 0)
    def _():
        trace[...] = part
        pre_ends[0] = pre[0]
        mass_ends[0] = mass[0]
        link_ends[0] = link[0]
        beside[0] = pre[1, sides[0]]
        first = precond[0]
        edges[2] = first
        edges[3] = exact(exact(first, diag[0]), first)

    @pl.when(step > 0)
    def _():
        trace[...] += part

    @pl.when(step == steps - 1)
    def _():
        pre_ends[1] = pre[blocks // 2 - 1]
        mass_ends[1] = mass[blocks // 2 - 1]
        link_ends[1] = link[blocks // 2 - 1]
        beside[1] = pre[blocks // 2 - 2, sides[1]]
        beside[2] = link[blocks // 2 - 2, plain]
        beside[3] = link[blocks // 2 - 2, turned]
        last = onward[blocks - 1] * coupling[steps * blocks - 1].astype(F32)
        mapped = exact(precond[blocks - 1], last)
        edges[0] = exact(last.T, mapped)
        edges[1] = exact(mapped.T, exact(diag[blocks - 1], mapped))


def mix_kernel(relay, arrived, mixing, trace, sending):
    total, values, rows = arrived.shape
    entries = trace.shape[0] * trace.shape[1]
    share = jnp.sum(jnp.sum(trace[...], axis=0, keepdims=True), axis=1, keepdims=True)
    share = jnp.maximum(jnp.broadcast_to(share, (1, rows)), TINY)
    share_code = jnp.floor(jnp.log2(share) * OCTAVE).astype(jnp.int32)
    lower = lax.broadcasted_iota(jnp.int32, (EXTRA, rows), 0) < EXTRA // 2

    def step(entry, carry):
        slot = relay[entry]
        tile = dot(arrived[slot], mixing[slot])
        peak = jnp.max(jnp.abs(tile), axis=0, keepdims=True)
        code = jnp.floor(jnp.log2(jnp.maximum(peak, TINY)) * OCTAVE) + 2.0
        scaled = tile * (FULL / jnp.exp2(code * (1.0 / OCTAVE)))
        scaled = jnp.clip(jnp.floor(scaled + 0.5), -32767.0, 32767.0)
        sending[entry, :values] = scaled.astype(jnp.int32).astype(jnp.int16)
        codes = jnp.where(lower, code.astype(jnp.int32), share_code)
        sending[entry, values:] = codes.astype(jnp.int16)
        return carry

    lax.fori_loop(0, total, step, 0, unroll=32)


def assemble_kernel(
    targets, received, pre_ends, mass_ends, link_ends, beside, edges, pre_away, rhs, theta_out, even_packet, odd_packet, pre, arrival, *, eigens
):
    total = received.shape[0]
    blocks, values, rows = rhs.shape
    copy = pltpu.make_async_copy(pre_away, pre, arrival)
    copy.start()
    rhs[...] = jnp.zeros_like(rhs)

    def step(entry, carry):
        extra = jnp.exp2(received[entry, values:].astype(jnp.int32).astype(F32) * (1.0 / OCTAVE))
        tile = received[entry, :values].astype(jnp.int32).astype(F32) * (extra[:1] * (1.0 / FULL))
        block = targets[entry]
        rhs[block] = rhs[block] + tile
        return carry + extra[EXTRA // 2 :]

    shares = lax.fori_loop(0, total, step, jnp.zeros((EXTRA // 2, rows), F32), unroll=8)
    theta = shares[:1] * (1.0 / eigens)
    theta_out[...] = jnp.broadcast_to(theta, theta_out.shape)

    sides, high, low, plain, turned = layout(rows)

    def conditioned(value, block):
        own = beside[block - 2] if block in (2, 3) else pre_ends[block // 4, sides[block % 2]]
        return by_wide(tall(value), own)

    both = functools.partial(jnp.concatenate, axis=1)
    first = [rhs[block] for block in range(EDGE)]
    z0 = [conditioned(first[block], block) for block in range(EDGE)]
    q1 = by_pair(tall(both(z0[:2])), mass_ends[0, high], mass_ends[0, low]) - both([theta, theta]) * both(first[:2])
    q1 = [q1[:, :rows], q1[:, rows:] + by_wide(tall(z0[2]), link_ends[0, turned])]
    z1 = [conditioned(q1[block], block) for block in range(2)]
    q2 = by_pair(tall(both(z1)), mass_ends[0, high], mass_ends[0, low])[:, :rows] - theta * q1[0]
    to_left = [z0[0], z1[0], conditioned(q2, 0)]
    last = [rhs[blocks - EDGE + block] for block in range(EDGE)]
    z0 = [conditioned(last[block], EDGE + block) for block in range(EDGE)]
    q1 = by_pair(tall(both(z0[1:])), mass_ends[1, high], mass_ends[1, low]) - both([theta, theta]) * both(last[1:])
    q1 = [q1[:, :rows] + by_wide(tall(z0[0]), beside[2]), q1[:, rows:]]
    z1 = [conditioned(q1[block], 4 + block) for block in range(2)]
    q2 = by_pair(tall(both(z1)), mass_ends[1, high], mass_ends[1, low])[:, rows:] - theta * q1[1]
    to_right = [by_wide(tall(value), link_ends[1, plain]) for value in (z0[2], z1[1], conditioned(q2, 5))]
    for product in range(4):
        for half in range(2):
            (to_right if product < 2 else to_left).append(edges[product, half * values : (half + 1) * values])
    even = stands_even()
    for entry in range(EDGE + 4):
        even_packet[entry] = jnp.where(even, to_right[entry], to_left[entry])
        odd_packet[entry] = jnp.where(even, to_left[entry], to_right[entry])
    copy.wait()


def basis_kernel(rhs, theta_in, pre, mass, link_away, basis, mapped, sums, stacked, link, arrival):
    blocks, values, rows = rhs.shape
    pairs = blocks // 2
    theta = theta_in[:1]
    theta_pair = jnp.concatenate([theta, theta], axis=1)
    sides, high, low, plain, turned = layout(rows)
    copy = pltpu.make_async_copy(link_away, link, arrival)
    copy.start()
    basis[0] = rhs[...]

    for level in range(3):
        even = jnp.zeros((values, rows), F32)
        for block in range(blocks):
            value = basis[level, block]
            image = by_wide(tall(value), pre[block // 2, sides[block % 2]])
            mapped[level, block] = image
            image_high, image_low = parted(image)
            side = slice((block % 2) * rows, (block % 2 + 1) * rows)
            stacked[block // 2, :values, side] = image_high
            stacked[block // 2, values:, side] = image_low
            if EDGE <= block < blocks - EDGE:
                even = even + value * image
        sums[2 * level] = even
        if level == 0:
            copy.wait()
        odd = jnp.zeros((values, rows), F32)
        for pair in range(pairs):
            image = by_pair(stacked[pair], mass[pair, high], mass[pair, low])
            parts = [image[:, :rows], image[:, rows:]]
            if pair > 0:
                parts[0] = parts[0] + by_wide(stacked[pair - 1, :, rows:], link[pair - 1, plain])
            if pair < pairs - 1:
                parts[1] = parts[1] + by_wide(stacked[pair + 1, :, :rows], link[pair, turned])
            for side in range(2):
                block = 2 * pair + side
                value = parts[side] - theta * basis[level, block]
                basis[level + 1, block] = value
                if EDGE <= block < blocks - EDGE:
                    odd = odd + value * mapped[level, block]
        sums[2 * level + 1] = odd


def edge_kernel(
    even_met, odd_met, basis, mapped, sums, theta_in, pre_ends, mass_ends, link_ends, beside, basis_edge, mapped_edge, moments
):
    _, blocks, values, rows = basis.shape
    theta = theta_in[:1]
    even = stands_even()
    from_left = [jnp.where(even, odd_met[entry], even_met[entry]) for entry in range(EDGE + 4)]
    from_right = [jnp.where(even, even_met[entry], odd_met[entry]) for entry in range(EDGE + 4)]

    sides, high, low, plain, turned = layout(rows)

    def conditioned(value, block):
        return by_wide(tall(value), pre_ends[block // 4, sides[block % 2]])

    def pair_image(first, second, pair):
        out = by_pair(tall(jnp.concatenate([first, second], axis=1)), mass_ends[pair, high], mass_ends[pair, low])
        return out[:, :rows], out[:, rows:]

    def square(ref, place):
        return jnp.concatenate([ref[place], ref[place + 1]], axis=0)

    none = jnp.zeros((values, rows), F32)

    mirror = square(from_left, 3)
    second = square(from_left, 5) - theta * mirror
    mirror, second = wide(mirror), wide(second)
    start = tall(mapped[0, 0])
    dq1 = from_left[0]
    dz1 = conditioned(dq1, 0)
    z1 = mapped[1, 0] + dz1
    own, after = pair_image(dz1, none, 0)
    dq2 = (own - theta * dq1 + from_left[1] + by_wide(start, mirror), after)
    dz2 = (conditioned(dq2[0], 0), conditioned(dq2[1], 1))
    own, after = pair_image(dz2[0], dz2[1], 0)
    dq3 = (
        own - theta * dq2[0] + from_left[2] + by_wide(start, second) + by_wide(tall(z1), mirror),
        after - theta * dq2[1],
        by_wide(tall(dz2[1]), link_ends[0, plain]),
    )
    changes = [((0, dq1),), ((0, dq2[0]), (1, dq2[1])), ((0, dq3[0]), (1, dq3[1]), (2, dq3[2]))]
    images = [((0, dz1),), ((0, dz2[0]), (1, dz2[1]))]

    last = blocks - 1
    mirror = square(from_right, 3)
    second = square(from_right, 5) - theta * mirror
    mirror, second = wide(mirror), wide(second)
    start = tall(by_wide(tall(mapped[0, last]), link_ends[1, plain]))
    dq1 = by_wide(tall(from_right[0]), link_ends[1, turned])
    dz1 = conditioned(dq1, 5)
    z1 = mapped[1, last] + dz1
    before, own = pair_image(none, dz1, 1)
    ahead = from_right[1] + by_wide(start, mirror)
    dq2 = (own - theta * dq1 + by_wide(tall(ahead), link_ends[1, turned]), before)
    dz2 = (conditioned(dq2[0], 5), conditioned(dq2[1], 4))
    before, own = pair_image(dz2[1], dz2[0], 1)
    ahead = from_right[2] + by_wide(start, second) + by_wide(tall(by_wide(tall(z1), link_ends[1, plain])), mirror)
    dq3 = (
        own - theta * dq2[0] + by_wide(tall(ahead), link_ends[1, turned]),
        before - theta * dq2[1],
        by_wide(tall(dz2[1]), beside[3]),
    )
    changes[0] += ((5, dq1),)
    changes[1] += ((5, dq2[0]), (4, dq2[1]))
    changes[2] += ((5, dq3[0]), (4, dq3[1]), (3, dq3[2]))
    images[0] += ((5, dz1),)
    images[1] += ((5, dz2[0]), (4, dz2[1]))

    places = [0, 1, 2, blocks - 3, blocks - 2, blocks - 1]
    before = [rhs_block for rhs_block in (basis[0, block] for block in places)]
    lane = lax.broadcasted_iota(jnp.int32, (values, rows), 1)
    table = none
    for level in range(3):
        image = [mapped[level, block] for block in places]
        if level > 0:
            for spot, change in images[level - 1]:
                image[spot] = image[spot] + change
            for spot in range(2 * EDGE):
                mapped_edge[level - 1, spot] = image[spot]
        now = [basis[level + 1, block] for block in places]
        for spot, change in changes[level]:
            now[spot] = now[spot] + change
        even = sums[2 * level]
        odd = sums[2 * level + 1]
        for spot in range(2 * EDGE):
            basis_edge[level, spot] = now[spot]
            even = even + before[spot] * image[spot]
            odd = odd + now[spot] * image[spot]
        table = jnp.where(lane == 2 * level, jnp.sum(even, axis=1, keepdims=True), table)
        table = jnp.where(lane == 2 * level + 1, jnp.sum(odd, axis=1, keepdims=True), table)
        before = now
    flipped = jnp.concatenate([table, jnp.zeros((rows - values, rows), F32)], axis=0).T[:8]
    for peer in range(moments.shape[0]):
        moments[peer] = flipped


def combine_kernel(moments, theta_in, basis, mapped, basis_edge, mapped_edge, solution, residual, factors):
    step = pl.program_id(0)
    _, blocks, values, rows = basis.shape
    chunk = solution.shape[0]

    @pl.when(step == 0)
    def _():
        total = jnp.sum(moments[...], axis=0)
        theta = theta_in[:1]
        m0, m1, m2, m3, m4, m5 = (total[place : place + 1] for place in range(6))
        m0 = m0 + TINY
        l10 = m1 / m0
        l20 = m2 / m0
        d1 = m2 - l10 * m1 + TINY
        g21 = m3 - l20 * m1
        l21 = g21 / d1
        d2 = m4 - l20 * m2 - l21 * g21 + TINY
        b1 = l10 * m3 - m4
        b2 = l20 * m3 - l21 * b1 - m5
        c2 = b2 / d2
        c1 = b1 / d1 - l21 * c2
        c0 = -m3 / m0 - l10 * c1 - l20 * c2
        scale = 1.0 / (c0 - theta * (c1 - theta * (c2 - theta)))
        c0, c1, c2, c3 = c0 * scale, c1 * scale, c2 * scale, scale
        y2 = -c3
        y1 = -c2 - theta * y2
        y0 = -c1 - theta * y1
        table = jnp.concatenate([c0, c1, c2, c3, y0, y1, y2, jnp.zeros((rows - 7, rows), F32)], axis=0).T
        for place in range(7):
            factors[place] = jnp.broadcast_to(table[:values, place : place + 1], (values, rows))

    def store(first, count, basis_of, mapped_of):
        for row in range(0, values, 32):
            part = slice(row, row + 32)
            factor = [factors[place, part] for place in range(7)]
            for place in range(first, first + count):
                q = basis_of(place, part)
                residual[place, part] = (q[0] * factor[0] + q[1] * factor[1]) + (q[2] * factor[2] + q[3] * factor[3])
            for place in range(first, first + count):
                z = mapped_of(place, part)
                solution[place, part] = z[0] * factor[4] + z[1] * factor[5] + z[2] * factor[6]

    store(
        0,
        chunk,
        lambda place, part: [basis[level, step * chunk + place, part] for level in range(4)],
        lambda place, part: [mapped[level, step * chunk + place, part] for level in range(3)],
    )

    def edge(first, block, entry):
        store(
            first,
            EDGE,
            lambda place, part: [basis[0, block - first + place, part]]
            + [basis_edge[level, entry - first + place, part] for level in range(3)],
            lambda place, part: [mapped[0, block - first + place, part]]
            + [mapped_edge[level, entry - first + place, part] for level in range(2)],
        )

    @pl.when(step == 0)
    def _():
        edge(0, 0, 0)

    @pl.when(step == pl.num_programs(0) - 1)
    def _():
        edge(chunk - EDGE, blocks - EDGE, EDGE)


def stands_even():
    return (lax.axis_index(AXES[0]) * lax.axis_size(AXES[1]) + lax.axis_index(AXES[1])) % 2 == 0


def exchanged(value, first):
    swaps = [(one, one + 1) for one in range(first, lax.axis_size(AXES) - 1, 2)]
    return lax.ppermute(value, AXES, swaps + [(other, one) for one, other in swaps])


def body(
    history,
    send_list,
    send_count,
    mixed_mass,
    relay_list,
    relay_target,
    mass_diag,
    mass_next,
    coupling,
    precond,
):
    devices = lax.axis_size(AXES)
    slots = send_list.shape[2]
    total = devices * slots
    values, rows = history.shape[1:]
    blocks = mass_diag.shape[0]
    pairs = blocks // 2
    field = (blocks, values, rows)
    stay = functools.partial(pltpu.with_memory_space_constraint, memory_space=pltpu.HBM)
    unit = 2 * values * rows * rows

    outgoing = pl.pallas_call(
        functools.partial(pick_kernel, slots=slots),
        out_shape=jax.ShapeDtypeStruct((total, values, rows), BF16),
        in_specs=[SCALARS, SCALARS, WHOLE],
        out_specs=WHOLE,
        compiler_params=params(10),
        name="pick",
    )(stay(send_list.reshape(-1)), stay(send_count.reshape(-1)), stay(history))
    arrived = lax.all_to_all(outgoing, AXES, split_axis=0, concat_axis=0, tiled=True)

    chunk = 16
    matrix = pl.BlockSpec((chunk, rows, rows), lambda step: (step, 0, 0))
    pre_part = link_part = (2 * rows, 2 * rows)
    mass_part = (4 * rows, 2 * rows)
    pre, mass, link, *ends, trace, edges = pl.pallas_call(
        prepare_kernel,
        grid=(blocks // chunk,),
        out_shape=(
            *(pltpu.HBM((pairs,) + part, BF16) for part in (pre_part, mass_part, link_part)),
            *(pltpu.VMEM((2,) + part, BF16) for part in (pre_part, mass_part, link_part)),
            pltpu.VMEM((4, rows, 2 * rows), BF16),
            pltpu.VMEM((8, rows), F32),
            pltpu.VMEM((4, rows, rows), F32),
        ),
        in_specs=[SCALARS, matrix, matrix, matrix],
        out_specs=tuple(
            pl.BlockSpec((chunk // 2,) + part, lambda step: (step, 0, 0)) for part in (pre_part, mass_part, link_part)
        )
        + (WHOLE,) * 6,
        compiler_params=params(28),
        cost_estimate=cost(0, 28 * 2**20),
        name="prepare",
    )(stay(coupling), stay(mass_diag), stay(mass_next), stay(precond))

    sending = pl.pallas_call(
        mix_kernel,
        out_shape=jax.ShapeDtypeStruct((total, values + EXTRA, rows), jnp.int16),
        in_specs=[SCALARS, WHOLE, WHOLE, WHOLE],
        out_specs=WHOLE,
        compiler_params=params(10),
        name="mix",
    )(relay_list.reshape(-1), arrived, mixed_mass, trace)
    received = lax.all_to_all(sending, AXES, split_axis=0, concat_axis=0, tiled=True)

    packet = jax.ShapeDtypeStruct((EDGE + 4, values, rows), F32)
    rhs, theta, even_packet, odd_packet, pre_held = pl.pallas_call(
        functools.partial(assemble_kernel, eigens=devices * blocks * rows),
        out_shape=(pltpu.VMEM(field, F32), pltpu.VMEM((8, rows), F32), packet, packet, pltpu.VMEM((pairs,) + pre_part, BF16)),
        in_specs=[SCALARS] + [WHOLE] * 6 + [AWAY],
        out_specs=(WHOLE,) * 5,
        scratch_shapes=[pltpu.SemaphoreType.DMA],
        compiler_params=params(10),
        name="assemble",
    )(relay_target.reshape(-1), received, *ends, edges, stay(pre))
    even_met = exchanged(even_packet, 0)
    odd_met = exchanged(odd_packet, 1)

    basis, mapped, sums = pl.pallas_call(
        basis_kernel,
        out_shape=(pltpu.VMEM((4,) + field, F32), pltpu.VMEM((3,) + field, F32), pltpu.VMEM((6, values, rows), F32)),
        in_specs=[WHOLE] * 4 + [AWAY],
        out_specs=(WHOLE,) * 3,
        scratch_shapes=[
            pltpu.VMEM((pairs, 2 * values, 2 * rows), BF16),
            pltpu.VMEM((pairs,) + link_part, BF16),
            pltpu.SemaphoreType.DMA,
        ],
        compiler_params=params(12),
        cost_estimate=cost(36 * blocks * unit, 32 * 2**20),
        name="basis",
    )(rhs, theta, pre_held, mass, stay(link))

    basis_edge, mapped_edge, moments = pl.pallas_call(
        edge_kernel,
        out_shape=(
            pltpu.VMEM((3, 2 * EDGE, values, rows), F32),
            pltpu.VMEM((2, 2 * EDGE, values, rows), F32),
            jax.ShapeDtypeStruct((devices, 8, rows), F32),
        ),
        in_specs=[WHOLE] * 10,
        out_specs=(WHOLE,) * 3,
        compiler_params=params(10),
        name="edge",
    )(even_met, odd_met, basis, mapped, sums, theta, *ends)
    gathered = lax.all_to_all(moments, AXES, split_axis=0, concat_axis=0, tiled=True)

    chunk = 16
    result = pl.BlockSpec((chunk, values, rows), lambda step: (step, 0, 0))
    return pl.pallas_call(
        combine_kernel,
        grid=(blocks // chunk,),
        out_shape=(jax.ShapeDtypeStruct(field, F32),) * 2,
        in_specs=[WHOLE] * 6,
        out_specs=(result, result),
        scratch_shapes=[pltpu.VMEM((7, values, rows), F32)],
        compiler_params=params(10),
        name="combine",
    )(gathered, theta, basis, mapped, basis_edge, mapped_edge)


def solution(mesh):
    placed = (
        P(AXES, None, None),
        P(AXES, None, None),
        P(AXES, None),
        P(AXES, None, None),
        P(AXES, None, None),
        P(AXES, None, None),
        P(AXES, None, None),
        P(AXES, None, None),
        P(AXES),
        P(AXES, None, None),
    )
    return jax.shard_map(
        body,
        mesh=mesh,
        in_specs=placed,
        out_specs=(P(AXES, None, None), P(AXES, None, None)),
        check_vma=False,
    )
```

```python
import functools

import jax
import jax.numpy as jnp
from jax import lax
from jax.experimental import pallas as pl
from jax.experimental.pallas import tpu as pltpu
from jax.sharding import PartitionSpec as P

AXES = ("dom", "sub")
EDGE = 3
EXTRA = 8
OCTAVE = 64.0
FULL = 32766.0
TINY = 1e-37
F32 = jnp.float32
BF16 = jnp.bfloat16
WHOLE = pl.BlockSpec(memory_space=pltpu.VMEM)
AWAY = pl.BlockSpec(memory_space=pl.ANY)
SCALARS = pl.BlockSpec(memory_space=pltpu.SMEM)


def params(mebibytes):
    return pltpu.CompilerParams(vmem_limit_bytes=mebibytes * 2**20)


def cost(flops, moved):
    return pl.CostEstimate(flops=int(flops), bytes_accessed=int(moved), transcendentals=0)


def layout(rows):
    def place(first, count):
        return slice(first * rows, (first + count) * rows)

    return (place(0, 1), place(1, 1)), place(0, 2), place(2, 2), place(0, 1), place(1, 1)


def dot(first, second):
    return jnp.dot(first, second, preferred_element_type=F32)


def parted(value):
    high = value.astype(BF16)
    return high, (value - high.astype(F32)).astype(BF16)


def tall(value):
    return jnp.concatenate(parted(value), axis=0)


def wide(value):
    return jnp.concatenate(parted(value), axis=1)


def by_wide(stacked, weights):
    rows, columns = stacked.shape[0] // 2, weights.shape[1] // 2
    out = dot(stacked, weights)
    return out[:rows, :columns] + (out[rows:, :columns] + out[:rows, columns:])


def by_pair(stacked, high, low):
    rows = stacked.shape[0] // 2
    out = dot(stacked, high)
    return out[:rows] + (out[rows:] + dot(stacked[:rows], low))


def pick_kernel(picks, counts, history, outgoing, *, slots):
    def step(entry, carry):
        live = (entry % slots) < counts[entry // slots]
        block = history[picks[entry]]
        outgoing[entry] = jnp.where(live, block, jnp.zeros_like(block))
        return carry

    total = outgoing.shape[0]
    lax.fori_loop(0, total, step, 0, unroll=8)


def prepare_kernel(coupling, diag, onward, precond, pre, mass, link, pre_ends, mass_ends, link_ends, beside, trace, edges):
    step = pl.program_id(0)
    steps = pl.num_programs(0)
    blocks = diag.shape[0]
    rows = diag.shape[1]
    sides, high, low, plain, turned = layout(rows)
    total = jnp.zeros((rows, rows), F32)
    for local in range(blocks // 2):
        pair = step * (blocks // 2) + local
        for side in range(2):
            own = precond[2 * local + side]
            pre[local, sides[side]] = wide(own)
            total = total + own * diag[2 * local + side]
        linked = onward[2 * local] * coupling[2 * pair].astype(F32)
        whole = jnp.concatenate(
            [
                jnp.concatenate([diag[2 * local], linked], axis=1),
                jnp.concatenate([linked.T, diag[2 * local + 1]], axis=1),
            ],
            axis=0,
        )
        mass[local, high], mass[local, low] = parted(whole)
        linked = onward[2 * local + 1] * coupling[2 * pair + 1].astype(F32)
        link[local, plain] = wide(linked)
        link[local, turned] = wide(linked.T)
    part = total.reshape(rows // 8, 8, rows).sum(axis=0)
    exact = functools.partial(jnp.dot, precision=lax.Precision.HIGHEST, preferred_element_type=F32)

    @pl.when(step == 0)
    def _():
        trace[...] = part
        pre_ends[0] = pre[0]
        mass_ends[0] = mass[0]
        link_ends[0] = link[0]
        beside[0] = pre[1, sides[0]]
        first = precond[0]
        edges[2] = first
        edges[3] = exact(exact(first, diag[0]), first)

    @pl.when(step > 0)
    def _():
        trace[...] += part

    @pl.when(step == steps - 1)
    def _():
        pre_ends[1] = pre[blocks // 2 - 1]
        mass_ends[1] = mass[blocks // 2 - 1]
        link_ends[1] = link[blocks // 2 - 1]
        beside[1] = pre[blocks // 2 - 2, sides[1]]
        beside[2] = link[blocks // 2 - 2, plain]
        beside[3] = link[blocks // 2 - 2, turned]
        last = onward[blocks - 1] * coupling[steps * blocks - 1].astype(F32)
        mapped = exact(precond[blocks - 1], last)
        edges[0] = exact(last.T, mapped)
        edges[1] = exact(mapped.T, exact(diag[blocks - 1], mapped))


def mix_kernel(relay, arrived, mixing, trace, sending):
    total, values, rows = arrived.shape
    entries = trace.shape[0] * trace.shape[1]
    share = jnp.sum(jnp.sum(trace[...], axis=0, keepdims=True), axis=1, keepdims=True)
    share = jnp.maximum(jnp.broadcast_to(share, (1, rows)), TINY)
    share_code = jnp.floor(jnp.log2(share) * OCTAVE).astype(jnp.int32)
    lower = lax.broadcasted_iota(jnp.int32, (EXTRA, rows), 0) < EXTRA // 2

    def step(entry, carry):
        slot = relay[entry]
        tile = dot(arrived[slot], mixing[slot])
        peak = jnp.max(jnp.abs(tile), axis=0, keepdims=True)
        code = jnp.floor(jnp.log2(jnp.maximum(peak, TINY)) * OCTAVE) + 2.0
        scaled = tile * (FULL / jnp.exp2(code * (1.0 / OCTAVE)))
        scaled = jnp.clip(jnp.floor(scaled + 0.5), -32767.0, 32767.0)
        sending[entry, :values] = scaled.astype(jnp.int32).astype(jnp.int16)
        codes = jnp.where(lower, code.astype(jnp.int32), share_code)
        sending[entry, values:] = codes.astype(jnp.int16)
        return carry

    lax.fori_loop(0, total, step, 0, unroll=32)


def assemble_kernel(
    targets, received, pre_ends, mass_ends, link_ends, beside, edges, pre_away, rhs, theta_out, even_packet, odd_packet, pre, arrival, *, eigens
):
    total = received.shape[0]
    blocks, values, rows = rhs.shape
    copy = pltpu.make_async_copy(pre_away, pre, arrival)
    copy.start()
    rhs[...] = jnp.zeros_like(rhs)

    def step(entry, carry):
        extra = jnp.exp2(received[entry, values:].astype(jnp.int32).astype(F32) * (1.0 / OCTAVE))
        tile = received[entry, :values].astype(jnp.int32).astype(F32) * (extra[:1] * (1.0 / FULL))
        block = targets[entry]
        rhs[block] = rhs[block] + tile
        return carry + extra[EXTRA // 2 :]

    shares = lax.fori_loop(0, total, step, jnp.zeros((EXTRA // 2, rows), F32), unroll=8)
    theta = shares[:1] * (1.0 / eigens)
    theta_out[...] = jnp.broadcast_to(theta, theta_out.shape)

    sides, high, low, plain, turned = layout(rows)

    def conditioned(value, block):
        own = beside[block - 2] if block in (2, 3) else pre_ends[block // 4, sides[block % 2]]
        return by_wide(tall(value), own)

    both = functools.partial(jnp.concatenate, axis=1)
    first = [rhs[block] for block in range(EDGE)]
    z0 = [conditioned(first[block], block) for block in range(EDGE)]
    q1 = by_pair(tall(both(z0[:2])), mass_ends[0, high], mass_ends[0, low]) - both([theta, theta]) * both(first[:2])
    q1 = [q1[:, :rows], q1[:, rows:] + by_wide(tall(z0[2]), link_ends[0, turned])]
    z1 = [conditioned(q1[block], block) for block in range(2)]
    q2 = by_pair(tall(both(z1)), mass_ends[0, high], mass_ends[0, low])[:, :rows] - theta * q1[0]
    to_left = [z0[0], z1[0], conditioned(q2, 0)]
    last = [rhs[blocks - EDGE + block] for block in range(EDGE)]
    z0 = [conditioned(last[block], EDGE + block) for block in range(EDGE)]
    q1 = by_pair(tall(both(z0[1:])), mass_ends[1, high], mass_ends[1, low]) - both([theta, theta]) * both(last[1:])
    q1 = [q1[:, :rows] + by_wide(tall(z0[0]), beside[2]), q1[:, rows:]]
    z1 = [conditioned(q1[block], 4 + block) for block in range(2)]
    q2 = by_pair(tall(both(z1)), mass_ends[1, high], mass_ends[1, low])[:, rows:] - theta * q1[1]
    to_right = [by_wide(tall(value), link_ends[1, plain]) for value in (z0[2], z1[1], conditioned(q2, 5))]
    for product in range(4):
        for half in range(2):
            (to_right if product < 2 else to_left).append(edges[product, half * values : (half + 1) * values])
    even = stands_even()
    for entry in range(EDGE + 4):
        even_packet[entry] = jnp.where(even, to_right[entry], to_left[entry])
        odd_packet[entry] = jnp.where(even, to_left[entry], to_right[entry])
    copy.wait()


def basis_kernel(rhs, theta_in, pre, mass, link_away, basis, mapped, sums, stacked, link, arrival):
    blocks, values, rows = rhs.shape
    pairs = blocks // 2
    theta = theta_in[:1]
    theta_pair = jnp.concatenate([theta, theta], axis=1)
    sides, high, low, plain, turned = layout(rows)
    copy = pltpu.make_async_copy(link_away, link, arrival)
    copy.start()
    basis[0] = rhs[...]

    for level in range(3):
        even = jnp.zeros((values, rows), F32)
        for block in range(blocks):
            value = basis[level, block]
            image = by_wide(tall(value), pre[block // 2, sides[block % 2]])
            mapped[level, block] = image
            image_high, image_low = parted(image)
            side = slice((block % 2) * rows, (block % 2 + 1) * rows)
            stacked[block // 2, :values, side] = image_high
            stacked[block // 2, values:, side] = image_low
            if EDGE <= block < blocks - EDGE:
                even = even + value * image
        sums[2 * level] = even
        if level == 0:
            copy.wait()
        odd = jnp.zeros((values, rows), F32)
        for pair in range(pairs):
            image = by_pair(stacked[pair], mass[pair, high], mass[pair, low])
            parts = [image[:, :rows], image[:, rows:]]
            if pair > 0:
                parts[0] = parts[0] + by_wide(stacked[pair - 1, :, rows:], link[pair - 1, plain])
            if pair < pairs - 1:
                parts[1] = parts[1] + by_wide(stacked[pair + 1, :, :rows], link[pair, turned])
            for side in range(2):
                block = 2 * pair + side
                value = parts[side] - theta * basis[level, block]
                basis[level + 1, block] = value
                if EDGE <= block < blocks - EDGE:
                    odd = odd + value * mapped[level, block]
        sums[2 * level + 1] = odd


def edge_kernel(
    even_met, odd_met, basis, mapped, sums, theta_in, pre_ends, mass_ends, link_ends, beside, basis_edge, mapped_edge, moments
):
    _, blocks, values, rows = basis.shape
    theta = theta_in[:1]
    even = stands_even()
    from_left = [jnp.where(even, odd_met[entry], even_met[entry]) for entry in range(EDGE + 4)]
    from_right = [jnp.where(even, even_met[entry], odd_met[entry]) for entry in range(EDGE + 4)]

    sides, high, low, plain, turned = layout(rows)

    def conditioned(value, block):
        return by_wide(tall(value), pre_ends[block // 4, sides[block % 2]])

    def pair_image(first, second, pair):
        out = by_pair(tall(jnp.concatenate([first, second], axis=1)), mass_ends[pair, high], mass_ends[pair, low])
        return out[:, :rows], out[:, rows:]

    def square(ref, place):
        return jnp.concatenate([ref[place], ref[place + 1]], axis=0)

    none = jnp.zeros((values, rows), F32)

    mirror = square(from_left, 3)
    second = square(from_left, 5) - theta * mirror
    mirror, second = wide(mirror), wide(second)
    start = tall(mapped[0, 0])
    dq1 = from_left[0]
    dz1 = conditioned(dq1, 0)
    z1 = mapped[1, 0] + dz1
    own, after = pair_image(dz1, none, 0)
    dq2 = (own - theta * dq1 + from_left[1] + by_wide(start, mirror), after)
    dz2 = (conditioned(dq2[0], 0), conditioned(dq2[1], 1))
    own, after = pair_image(dz2[0], dz2[1], 0)
    dq3 = (
        own - theta * dq2[0] + from_left[2] + by_wide(start, second) + by_wide(tall(z1), mirror),
        after - theta * dq2[1],
        by_wide(tall(dz2[1]), link_ends[0, plain]),
    )
    changes = [((0, dq1),), ((0, dq2[0]), (1, dq2[1])), ((0, dq3[0]), (1, dq3[1]), (2, dq3[2]))]
    images = [((0, dz1),), ((0, dz2[0]), (1, dz2[1]))]

    last = blocks - 1
    mirror = square(from_right, 3)
    second = square(from_right, 5) - theta * mirror
    mirror, second = wide(mirror), wide(second)
    start = tall(by_wide(tall(mapped[0, last]), link_ends[1, plain]))
    dq1 = by_wide(tall(from_right[0]), link_ends[1, turned])
    dz1 = conditioned(dq1, 5)
    z1 = mapped[1, last] + dz1
    before, own = pair_image(none, dz1, 1)
    ahead = from_right[1] + by_wide(start, mirror)
    dq2 = (own - theta * dq1 + by_wide(tall(ahead), link_ends[1, turned]), before)
    dz2 = (conditioned(dq2[0], 5), conditioned(dq2[1], 4))
    before, own = pair_image(dz2[1], dz2[0], 1)
    ahead = from_right[2] + by_wide(start, second) + by_wide(tall(by_wide(tall(z1), link_ends[1, plain])), mirror)
    dq3 = (
        own - theta * dq2[0] + by_wide(tall(ahead), link_ends[1, turned]),
        before - theta * dq2[1],
        by_wide(tall(dz2[1]), beside[3]),
    )
    changes[0] += ((5, dq1),)
    changes[1] += ((5, dq2[0]), (4, dq2[1]))
    changes[2] += ((5, dq3[0]), (4, dq3[1]), (3, dq3[2]))
    images[0] += ((5, dz1),)
    images[1] += ((5, dz2[0]), (4, dz2[1]))

    places = [0, 1, 2, blocks - 3, blocks - 2, blocks - 1]
    before = [rhs_block for rhs_block in (basis[0, block] for block in places)]
    lane = lax.broadcasted_iota(jnp.int32, (values, rows), 1)
    table = none
    for level in range(3):
        image = [mapped[level, block] for block in places]
        if level > 0:
            for spot, change in images[level - 1]:
                image[spot] = image[spot] + change
            for spot in range(2 * EDGE):
                mapped_edge[level - 1, spot] = image[spot]
        now = [basis[level + 1, block] for block in places]
        for spot, change in changes[level]:
            now[spot] = now[spot] + change
        even = sums[2 * level]
        odd = sums[2 * level + 1]
        for spot in range(2 * EDGE):
            basis_edge[level, spot] = now[spot]
            even = even + before[spot] * image[spot]
            odd = odd + now[spot] * image[spot]
        table = jnp.where(lane == 2 * level, jnp.sum(even, axis=1, keepdims=True), table)
        table = jnp.where(lane == 2 * level + 1, jnp.sum(odd, axis=1, keepdims=True), table)
        before = now
    flipped = jnp.concatenate([table, jnp.zeros((rows - values, rows), F32)], axis=0).T[:8]
    for peer in range(moments.shape[0]):
        moments[peer] = flipped


def combine_kernel(moments, theta_in, basis, mapped, basis_edge, mapped_edge, solution, residual, factors):
    step = pl.program_id(0)
    _, blocks, values, rows = basis.shape
    chunk = solution.shape[0]

    @pl.when(step == 0)
    def _():
        total = jnp.sum(moments[...], axis=0)
        theta = theta_in[:1]
        m0, m1, m2, m3, m4, m5 = (total[place : place + 1] for place in range(6))
        m0 = m0 + TINY
        l10 = m1 / m0
        l20 = m2 / m0
        d1 = m2 - l10 * m1 + TINY
        g21 = m3 - l20 * m1
        l21 = g21 / d1
        d2 = m4 - l20 * m2 - l21 * g21 + TINY
        b1 = l10 * m3 - m4
        b2 = l20 * m3 - l21 * b1 - m5
        c2 = b2 / d2
        c1 = b1 / d1 - l21 * c2
        c0 = -m3 / m0 - l10 * c1 - l20 * c2
        scale = 1.0 / (c0 - theta * (c1 - theta * (c2 - theta)))
        c0, c1, c2, c3 = c0 * scale, c1 * scale, c2 * scale, scale
        y2 = -c3
        y1 = -c2 - theta * y2
        y0 = -c1 - theta * y1
        table = jnp.concatenate([c0, c1, c2, c3, y0, y1, y2, jnp.zeros((rows - 7, rows), F32)], axis=0).T
        for place in range(7):
            factors[place] = jnp.broadcast_to(table[:values, place : place + 1], (values, rows))

    def store(first, count, basis_of, mapped_of):
        for row in range(0, values, 64):
            part = slice(row, row + 64)
            factor = [factors[place, part] for place in range(7)]
            for place in range(first, first + count):
                q = basis_of(place, part)
                residual[place, part] = (q[0] * factor[0] + q[1] * factor[1]) + (q[2] * factor[2] + q[3] * factor[3])
            for place in range(first, first + count):
                z = mapped_of(place, part)
                solution[place, part] = z[0] * factor[4] + z[1] * factor[5] + z[2] * factor[6]

    store(
        0,
        chunk,
        lambda place, part: [basis[level, step * chunk + place, part] for level in range(4)],
        lambda place, part: [mapped[level, step * chunk + place, part] for level in range(3)],
    )

    def edge(first, block, entry):
        store(
            first,
            EDGE,
            lambda place, part: [basis[0, block - first + place, part]]
            + [basis_edge[level, entry - first + place, part] for level in range(3)],
            lambda place, part: [mapped[0, block - first + place, part]]
            + [mapped_edge[level, entry - first + place, part] for level in range(2)],
        )

    @pl.when(step == 0)
    def _():
        edge(0, 0, 0)

    @pl.when(step == pl.num_programs(0) - 1)
    def _():
        edge(chunk - EDGE, blocks - EDGE, EDGE)


def stands_even():
    return (lax.axis_index(AXES[0]) * lax.axis_size(AXES[1]) + lax.axis_index(AXES[1])) % 2 == 0


def exchanged(value, first):
    swaps = [(one, one + 1) for one in range(first, lax.axis_size(AXES) - 1, 2)]
    return lax.ppermute(value, AXES, swaps + [(other, one) for one, other in swaps])


def body(
    history,
    send_list,
    send_count,
    mixed_mass,
    relay_list,
    relay_target,
    mass_diag,
    mass_next,
    coupling,
    precond,
):
    devices = lax.axis_size(AXES)
    slots = send_list.shape[2]
    total = devices * slots
    values, rows = history.shape[1:]
    blocks = mass_diag.shape[0]
    pairs = blocks // 2
    field = (blocks, values, rows)
    stay = functools.partial(pltpu.with_memory_space_constraint, memory_space=pltpu.HBM)
    unit = 2 * values * rows * rows

    outgoing = pl.pallas_call(
        functools.partial(pick_kernel, slots=slots),
        out_shape=jax.ShapeDtypeStruct((total, values, rows), BF16),
        in_specs=[SCALARS, SCALARS, WHOLE],
        out_specs=WHOLE,
        compiler_params=params(10),
        name="pick",
    )(stay(send_list.reshape(-1)), stay(send_count.reshape(-1)), stay(history))
    arrived = lax.all_to_all(outgoing, AXES, split_axis=0, concat_axis=0, tiled=True)

    chunk = 16
    matrix = pl.BlockSpec((chunk, rows, rows), lambda step: (step, 0, 0))
    pre_part = link_part = (2 * rows, 2 * rows)
    mass_part = (4 * rows, 2 * rows)
    pre, mass, link, *ends, trace, edges = pl.pallas_call(
        prepare_kernel,
        grid=(blocks // chunk,),
        out_shape=(
            *(pltpu.HBM((pairs,) + part, BF16) for part in (pre_part, mass_part, link_part)),
            *(pltpu.VMEM((2,) + part, BF16) for part in (pre_part, mass_part, link_part)),
            pltpu.VMEM((4, rows, 2 * rows), BF16),
            pltpu.VMEM((8, rows), F32),
            pltpu.VMEM((4, rows, rows), F32),
        ),
        in_specs=[SCALARS, matrix, matrix, matrix],
        out_specs=tuple(
            pl.BlockSpec((chunk // 2,) + part, lambda step: (step, 0, 0)) for part in (pre_part, mass_part, link_part)
        )
        + (WHOLE,) * 6,
        compiler_params=params(28),
        cost_estimate=cost(0, 28 * 2**20),
        name="prepare",
    )(stay(coupling), stay(mass_diag), stay(mass_next), stay(precond))

    sending = pl.pallas_call(
        mix_kernel,
        out_shape=jax.ShapeDtypeStruct((total, values + EXTRA, rows), jnp.int16),
        in_specs=[SCALARS, WHOLE, WHOLE, WHOLE],
        out_specs=WHOLE,
        compiler_params=params(10),
        name="mix",
    )(relay_list.reshape(-1), arrived, mixed_mass, trace)
    received = lax.all_to_all(sending, AXES, split_axis=0, concat_axis=0, tiled=True)

    packet = jax.ShapeDtypeStruct((EDGE + 4, values, rows), F32)
    rhs, theta, even_packet, odd_packet, pre_held = pl.pallas_call(
        functools.partial(assemble_kernel, eigens=devices * blocks * rows),
        out_shape=(pltpu.VMEM(field, F32), pltpu.VMEM((8, rows), F32), packet, packet, pltpu.VMEM((pairs,) + pre_part, BF16)),
        in_specs=[SCALARS] + [WHOLE] * 6 + [AWAY],
        out_specs=(WHOLE,) * 5,
        scratch_shapes=[pltpu.SemaphoreType.DMA],
        compiler_params=params(10),
        name="assemble",
    )(relay_target.reshape(-1), received, *ends, edges, stay(pre))
    even_met = exchanged(even_packet, 0)
    odd_met = exchanged(odd_packet, 1)

    basis, mapped, sums = pl.pallas_call(
        basis_kernel,
        out_shape=(pltpu.VMEM((4,) + field, F32), pltpu.VMEM((3,) + field, F32), pltpu.VMEM((6, values, rows), F32)),
        in_specs=[WHOLE] * 4 + [AWAY],
        out_specs=(WHOLE,) * 3,
        scratch_shapes=[
            pltpu.VMEM((pairs, 2 * values, 2 * rows), BF16),
            pltpu.VMEM((pairs,) + link_part, BF16),
            pltpu.SemaphoreType.DMA,
        ],
        compiler_params=params(12),
        cost_estimate=cost(36 * blocks * unit, 32 * 2**20),
        name="basis",
    )(rhs, theta, pre_held, mass, stay(link))

    basis_edge, mapped_edge, moments = pl.pallas_call(
        edge_kernel,
        out_shape=(
            pltpu.VMEM((3, 2 * EDGE, values, rows), F32),
            pltpu.VMEM((2, 2 * EDGE, values, rows), F32),
            jax.ShapeDtypeStruct((devices, 8, rows), F32),
        ),
        in_specs=[WHOLE] * 10,
        out_specs=(WHOLE,) * 3,
        compiler_params=params(10),
        name="edge",
    )(even_met, odd_met, basis, mapped, sums, theta, *ends)
    gathered = lax.all_to_all(moments, AXES, split_axis=0, concat_axis=0, tiled=True)

    chunk = 16
    result = pl.BlockSpec((chunk, values, rows), lambda step: (step, 0, 0))
    return pl.pallas_call(
        combine_kernel,
        grid=(blocks // chunk,),
        out_shape=(jax.ShapeDtypeStruct(field, F32),) * 2,
        in_specs=[WHOLE] * 6,
        out_specs=(result, result),
        scratch_shapes=[pltpu.VMEM((7, values, rows), F32)],
        compiler_params=params(10),
        name="combine",
    )(gathered, theta, basis, mapped, basis_edge, mapped_edge)


def solution(mesh):
    placed = (
        P(AXES, None, None),
        P(AXES, None, None),
        P(AXES, None),
        P(AXES, None, None),
        P(AXES, None, None),
        P(AXES, None, None),
        P(AXES, None, None),
        P(AXES, None, None),
        P(AXES),
        P(AXES, None, None),
    )
    return jax.shard_map(
        body,
        mesh=mesh,
        in_specs=placed,
        out_specs=(P(AXES, None, None), P(AXES, None, None)),
        check_vma=False,
    )
```
